128 devices in a mesh: fsdp: 16 (over y, x), tp: 8 (over z, core).
Axes of the slice: x: 4, y: 4, z: 4, core: 2. Of those that a mesh axis runs over, the one named last changes fastest.
Arguments:
- gradient: bfloat16 [8192, 10240], P(('fsdp', 'tp'))
- owner: int32 [80], replicated, may hold values from 0 to 127, as said below
- l_stat: float32 [128, 1024, 1024], P(('fsdp', 'tp'))
- r_stat: float32 [128, 1024, 1024], P(('fsdp', 'tp'))
- l_root: bfloat16 [128, 1024, 1024], P(('fsdp', 'tp'))
- r_root: bfloat16 [128, 1024, 1024], P(('fsdp', 'tp'))
Outputs:
- update: bfloat16 [8192, 10240], P('fsdp', 'tp')
- new_left: float32 [128, 1024, 1024], P(('fsdp', 'tp'))
- new_right: float32 [128, 1024, 1024], P(('fsdp', 'tp'))
The draws below stay inside these ranges and needn't reach their ends.
Inputs may be any that keep to these rules, and one draw needn't show every extreme that they name: `owner`: no two blocks name the same slot; slot g lies on device g, devices numbered fsdp index times the size of tp plus tp index. Among the 10 blocks of one row of blocks at most 1 have owners with the same fsdp index, and some row of blocks has exactly 1 such.
All inputs are finite; a program needn't handle non-finite values.
Results may differ from the reference program's by a relative error of at most 0.0049.
Values may be sent and summed in bfloat16 or wider, within the bound.
A program may use at most 128 MiB of HBM per device.

```python
import math
import jax
import jax.numpy as jnp
from jax import lax

D = 8192
QKV = 10240
BLOCK = 1024
BLOCKS = 80
SLOT_DEV = 1
SLOTS = 128
N_FSDP = 16
N_TP = 8


def symmetric_draw(key, diag_low, diag_high, off_scale):
    key_diag, key_off = jax.random.split(key)
    diagonal = jnp.exp(jax.random.uniform(key_diag, (SLOTS, BLOCK), minval=math.log(diag_low), maxval=math.log(diag_high)))
    noise = jax.random.normal(key_off, (SLOTS, BLOCK, BLOCK), dtype=jnp.float32) * (off_scale / math.sqrt(BLOCK))
    return (noise + jnp.swapaxes(noise, 1, 2)) * 0.7071 + diagonal[:, :, None] * jnp.eye(BLOCK, dtype=jnp.float32)[None]


def draw_l_root(key, part):
    key = jax.random.fold_in(key, 11)
    return symmetric_draw(key, 0.4, 2.5, 0.5).astype(jnp.bfloat16)


def draw_r_root(key, part):
    key = jax.random.fold_in(key, 12)
    return symmetric_draw(key, 0.4, 2.5, 0.5).astype(jnp.bfloat16)


def draw_l_stat(key, part):
    key = jax.random.fold_in(key, 13)
    return symmetric_draw(key, 0.3, 3.0, 0.3)


def draw_r_stat(key, part):
    key = jax.random.fold_in(key, 14)
    return symmetric_draw(key, 0.3, 3.0, 0.3)


def draw_gradient(key, part):
    key = jax.random.fold_in(key, 15)
    key_rows, key_cols, key_vals = jax.random.split(key, 3)
    row_scale = jnp.exp(jax.random.uniform(key_rows, (D, 1), minval=-1.15, maxval=1.15))
    col_scale = jnp.exp(jax.random.uniform(key_cols, (1, QKV), minval=-1.15, maxval=1.15))
    values = jax.random.normal(key_vals, (D, QKV), dtype=jnp.float32)
    return (values * row_scale * col_scale * (1.0 / 32.0)).astype(jnp.bfloat16)


def draw_owner(key, part):
    key = jax.random.fold_in(key, 16)
    key_shift, key_label, key_local = jax.random.split(key, 3)
    shift_amount = jax.random.randint(key_shift, (), 0, N_FSDP)
    relabel = jax.random.permutation(key_label, N_FSDP)
    local_keys = jax.random.split(key_local, N_FSDP)
    local_orders = jax.vmap(lambda single: jax.random.permutation(single, N_TP * SLOT_DEV))(local_keys)
    block_ids = jnp.arange(BLOCKS, dtype=jnp.int32)
    fsdp_of = relabel[(block_ids + shift_amount) % N_FSDP]
    local_slot = local_orders[fsdp_of, block_ids // N_FSDP]
    return (fsdp_of * (N_TP * SLOT_DEV) + local_slot).astype(jnp.int32)


def setup_inputs(seed: int = 0) -> dict:
    arg_keys = jax.random.split(jax.random.key(seed), 7)
    gradient = draw_gradient(jax.random.fold_in(arg_keys[6], 71), 0)
    owner = draw_owner(jax.random.fold_in(arg_keys[6], 71), 0)
    l_stat = draw_l_stat(jax.random.fold_in(arg_keys[6], 71), 0)
    r_stat = draw_r_stat(jax.random.fold_in(arg_keys[6], 71), 0)
    l_root = draw_l_root(jax.random.fold_in(arg_keys[6], 71), 0)
    r_root = draw_r_root(jax.random.fold_in(arg_keys[6], 71), 0)
    return dict(gradient=gradient, owner=owner, l_stat=l_stat, r_stat=r_stat, l_root=l_root, r_root=r_root)


decay = 0.9
eps = 1e-06

def one_block(items):
    grad_block, left_old, right_old, left_inv, right_inv = items
    left_new = decay * left_old + (1.0 - decay) * jnp.dot(grad_block, grad_block.T, preferred_element_type=jnp.float32)
    right_new = decay * right_old + (1.0 - decay) * jnp.dot(grad_block.T, grad_block, preferred_element_type=jnp.float32)
    halfway = jnp.dot(left_inv, grad_block, preferred_element_type=jnp.float32).astype(jnp.bfloat16)
    product = jnp.dot(halfway, right_inv, preferred_element_type=jnp.float32)
    factor = lax.rsqrt(jnp.mean(product * product) + eps)
    return ((product * factor).astype(jnp.bfloat16), left_new, right_new)

def reference(gradient, owner, l_stat, r_stat, l_root, r_root):
    row_count = D // BLOCK
    column_count = QKV // BLOCK
    blocks = gradient.reshape(row_count, BLOCK, column_count, BLOCK).transpose(0, 2, 1, 3).reshape(row_count * column_count, BLOCK, BLOCK)
    scaled_blocks, left_blocks, right_blocks = lax.map(one_block, (blocks, l_stat[owner], r_stat[owner], l_root[owner], r_root[owner]))
    new_left = (decay * l_stat).at[owner].set(left_blocks)
    new_right = (decay * r_stat).at[owner].set(right_blocks)
    update = scaled_blocks.reshape(row_count, column_count, BLOCK, BLOCK).transpose(0, 2, 1, 3).reshape(D, QKV)
    return (update, new_left, new_right)
```

```python
import functools

import jax
import jax.numpy as jnp
from jax import lax
from jax.experimental import pallas as pl
from jax.experimental.pallas import tpu as pltpu
from jax.sharding import PartitionSpec as P

MESH = pl.DeviceIdType.MESH
VMEM = pltpu.VMEM
DMA = pltpu.SemaphoreType.DMA

decay = 0.9
eps = 1e-06

BLOCK = 1024
COLS = 10
N_F = 16
N_T = 8
RING = 4
ROWS = 64
CHUNKS = 4
CW = BLOCK // CHUNKS
RW = ROWS // CHUNKS
OUT_COLS = 1280
Q = 256

F_STEPS = [(2, 2), (1, 2), (2, 1), (3, 2), (2, 3), (1, 1), (3, 3), (1, 3), (3, 1), (0, 2), (2, 0), (0, 1), (1, 0), (0, 3), (3, 0)]
T_STEPS = [(2, 0), (2, 1), (1, 0), (3, 0), (1, 1), (3, 1), (0, 1)]


def fsdp_at(f, step):
    y = lax.rem(f // RING + step[0], RING)
    x = lax.rem(lax.rem(f, RING) + step[1], RING)
    return y * RING + x


def tp_at(t, step):
    z = lax.rem(t // 2 + step[0], RING)
    return z * 2 + lax.rem(lax.rem(t, 2) + step[1], 2)


def greet(f, t):
    barrier = pltpu.get_barrier_semaphore()
    for step in F_STEPS:
        pl.semaphore_signal(barrier, inc=1, device_id=(fsdp_at(f, step), t), device_id_type=MESH)
    for step in T_STEPS:
        pl.semaphore_signal(barrier, inc=1, device_id=(f, tp_at(t, step)), device_id_type=MESH)
    pl.semaphore_wait(barrier, len(F_STEPS) + len(T_STEPS))


def send(src, dst, send_sem, recv_sem, f, t):
    copy = pltpu.make_async_remote_copy(
        src_ref=src, dst_ref=dst, send_sem=send_sem, recv_sem=recv_sem, device_id=(f, t), device_id_type=MESH
    )
    copy.start()
    return copy


def forward_kernel(owner_ref, g_hbm, o_ref, g_ref, g_sem, s1, r1a, r1b, r1c, r1d, s2, ss1, rs1, ss2, rs2):
    f, t = lax.axis_index("fsdp"), lax.axis_index("tp")
    r1 = (r1a, r1b, r1c, r1d)
    half_row, half = f // 2, lax.rem(f, 2)
    line = half_row * COLS
    owners = [owner_ref[line + c] // N_T for c in range(COLS)]

    def column_of(fsdp):
        col = jnp.int32(0)
        for c in range(COLS):
            col = jnp.where(owners[c] == fsdp, c, col)
        return col

    def piece(col, k):
        return g_ref[col, :, k * CW : (k + 1) * CW]

    loads = []
    for c in range(COLS):
        load = pltpu.make_async_copy(g_hbm.at[:, c * BLOCK : (c + 1) * BLOCK], g_ref.at[c], g_sem.at[c])
        load.start()
        loads.append(load)
    greet(f, t)
    for load in loads:
        load.wait()
    dests = [fsdp_at(f, s) for s in F_STEPS]
    cols = [column_of(d) for d in dests]
    mine = column_of(f)
    sent = []
    for k in range(CHUNKS):
        for i, d in enumerate(dests):
            s1[k, i] = piece(cols[i], k)
            sent.append(send(s1.at[k, i], r1[k].at[half_row, half], ss1.at[k, i], rs1.at[k, i], d, t))
        r1[k][half_row, half] = piece(mine, k)

    def row_of(tp):
        slot = f * N_T + tp

        def body(j, row):
            return jnp.where(owner_ref[j] == slot, j // COLS, row)

        return lax.fori_loop(0, COLS * N_T, body, jnp.int32(0))

    tps = [tp_at(t, s) for s in T_STEPS]
    rows = [row_of(d) for d in tps]
    my_row = row_of(t)
    passed = []
    for k in range(CHUNKS):
        for c in sent[k * len(dests) : (k + 1) * len(dests)]:
            c.wait_recv()
        for i, d in enumerate(tps):
            s2[k, i] = r1[k][rows[i]]
            passed.append(send(s2.at[k, i], o_ref.at[k, :, t], ss2.at[k, i], rs2.at[k, i], f, d))
        o_ref[k, :, t] = r1[k][my_row]
    for c in passed:
        c.wait_recv()
    for c in sent + passed:
        c.wait_send()


def forward(owner, gradient):
    return pl.pallas_call(
        forward_kernel,
        out_shape=jax.ShapeDtypeStruct((CHUNKS, 2, N_T, ROWS, CW), jnp.bfloat16),
        in_specs=[pl.BlockSpec(memory_space=pltpu.SMEM), pl.BlockSpec(memory_space=pl.ANY)],
        out_specs=pl.BlockSpec(memory_space=VMEM),
        scratch_shapes=[VMEM((COLS, ROWS, BLOCK), jnp.bfloat16), DMA((COLS,))]
        + [VMEM((CHUNKS, len(F_STEPS), ROWS, CW), jnp.bfloat16)]
        + [VMEM((N_F // 2, 2, ROWS, CW), jnp.bfloat16)] * CHUNKS
        + [VMEM((CHUNKS, len(T_STEPS), 2, ROWS, CW), jnp.bfloat16)]
        + [DMA((CHUNKS, len(F_STEPS)))] * 2
        + [DMA((CHUNKS, len(T_STEPS)))] * 2,
        compiler_params=pltpu.CompilerParams(collective_id=0, has_side_effects=True, vmem_limit_bytes=32 << 20),
        name="forward",
    )(owner, gradient)


def root_kernel(g_ref, l_ref, r_ref, o_ref, half, full):
    for k in range(CHUNKS):
        g = g_ref[k].reshape(BLOCK, CW)
        for i in range(4):
            rows = pl.ds(i * 256, 256)
            half[rows, k * CW : (k + 1) * CW] = jnp.dot(l_ref[rows], g, preferred_element_type=jnp.float32).astype(jnp.bfloat16)
    total = jnp.zeros((8, 256), jnp.float32)
    for i in range(4):
        rows = pl.ds(i * 256, 256)
        for j in range(4):
            cols = pl.ds(j * 256, 256)
            p = jnp.dot(half[rows], r_ref[:, cols], preferred_element_type=jnp.float32)
            full[rows, cols] = p
            total += jnp.sum((p * p).reshape(32, 8, 256), axis=0)
    factor = lax.rsqrt(jnp.sum(total) / (BLOCK * BLOCK) + eps)
    for i in range(16):
        rows = pl.ds(i * 64, 64)
        o_ref[i // 8, i % 8] = (full[rows] * factor).astype(jnp.bfloat16)


def roots(g, l_root, r_root):
    return pl.pallas_call(
        root_kernel,
        out_shape=jax.ShapeDtypeStruct((2, N_T, ROWS, BLOCK), jnp.bfloat16),
        in_specs=[pl.BlockSpec(memory_space=VMEM)] * 3,
        out_specs=pl.BlockSpec(memory_space=VMEM),
        scratch_shapes=[VMEM((BLOCK, BLOCK), jnp.bfloat16), VMEM((BLOCK, BLOCK), jnp.float32)],
        compiler_params=pltpu.CompilerParams(vmem_limit_bytes=32 << 20),
        name="roots",
    )(g, l_root, r_root)


STAT_ROWS = 128


def stat_kernel(owner_ref, g_ref, l_ref, r_ref, nl_ref, nr_ref):
    i = pl.program_id(0)
    me = lax.axis_index("fsdp") * N_T + lax.axis_index("tp")
    has = lax.fori_loop(0, COLS * N_T, lambda j, n: n + (owner_ref[j] == me).astype(jnp.int32), jnp.int32(0)) > 0
    left = jnp.zeros((STAT_ROWS, BLOCK), jnp.float32)
    for k in range(CHUNKS):
        g = g_ref[k].reshape(BLOCK, CW)
        rows = g_ref[k, i // 4, pl.ds(lax.rem(i, 4) * 2, 2)].reshape(STAT_ROWS, CW)
        left += lax.dot_general(rows, g, (((1,), (1,)), ((), ())), preferred_element_type=jnp.float32)
    nl_ref[...] = decay * l_ref[...] + jnp.where(has, (1.0 - decay) * left, 0.0)
    lane = pl.ds(pl.multiple_of(lax.rem(i, CW // STAT_ROWS) * STAT_ROWS, STAT_ROWS), STAT_ROWS)
    mine = g_ref[i // (CW // STAT_ROWS), :, :, :, lane].reshape(BLOCK, STAT_ROWS)
    for k in range(CHUNKS):
        right = lax.dot_general(
            mine, g_ref[k].reshape(BLOCK, CW), (((0,), (0,)), ((), ())), preferred_element_type=jnp.float32
        )
        cols = slice(k * CW, (k + 1) * CW)
        nr_ref[:, cols] = decay * r_ref[:, cols] + jnp.where(has, (1.0 - decay) * right, 0.0)


def stats(owner, g, l_stat, r_stat):
    block = pl.BlockSpec((STAT_ROWS, BLOCK), lambda i: (i, 0))
    return pl.pallas_call(
        stat_kernel,
        grid=(BLOCK // STAT_ROWS,),
        out_shape=[jax.ShapeDtypeStruct((BLOCK, BLOCK), jnp.float32)] * 2,
        in_specs=[pl.BlockSpec(memory_space=pltpu.SMEM), pl.BlockSpec(memory_space=VMEM), block, block],
        out_specs=[block, block],
        compiler_params=pltpu.CompilerParams(vmem_limit_bytes=32 << 20),
        name="stats",
    )(owner, g, l_stat, r_stat)


def backward_kernel(owner_ref, b_ref, o_ref, ra, rb, rc, rd, s2, xa, xb, xc, xd, s3, ss1, rs1, ss2, rs2, ss3, rs3):
    f, t = lax.axis_index("fsdp"), lax.axis_index("tp")
    r1, r2 = (ra, rb, rc, rd), (xa, xb, xc, xd)
    greet(f, t)
    tps = [tp_at(t, s) for s in T_STEPS]
    dests = [fsdp_at(f, s) for s in F_STEPS]
    n_t, n_f = len(tps), len(dests)
    spread = []
    for k in range(CHUNKS):
        rows = pl.ds(k * RW, RW)
        for i, d in enumerate(tps):
            spread.append(send(b_ref.at[:, d, rows], r1[k].at[t], ss1.at[k, i], rs1.at[k, i], f, d))
        r1[k][t] = b_ref[:, t, rows]

    def tp_of(fsdp):
        line = (fsdp // 2) * COLS
        tp = jnp.int32(0)
        for c in range(COLS):
            o = owner_ref[line + c]
            tp = jnp.where(o // N_T == f, lax.rem(o, N_T), tp)
        return tp

    slots = [tp_of(d) for d in dests]
    my_slot = tp_of(f)
    home = []
    for k in range(CHUNKS):
        for c in spread[k * n_t : (k + 1) * n_t]:
            c.wait_recv()
        for i, d in enumerate(dests):
            piece = r1[k][slots[i], lax.rem(d, 2)]
            for q in range(BLOCK // Q):
                s2[k, i, q] = piece[:, q * Q : (q + 1) * Q]
            home.append(send(s2.at[k, i], r2[k].at[f], ss2.at[k, i], rs2.at[k, i], d, t))
        piece = r1[k][my_slot, lax.rem(f, 2)]
        for q in range(BLOCK // Q):
            r2[k][f, q] = piece[:, q * Q : (q + 1) * Q]

    line = (f // 2) * COLS

    def parts_of(tp):
        parts = []
        for j in range(OUT_COLS // Q):
            chunk = tp * (OUT_COLS // Q) + j
            source = owner_ref[line + chunk // (BLOCK // Q)] // N_T
            parts.append((source, lax.rem(chunk, BLOCK // Q)))
        return parts

    parts = [parts_of(d) for d in tps]
    my_parts = parts_of(t)
    last = []
    for k in range(CHUNKS):
        for c in home[k * n_f : (k + 1) * n_f]:
            c.wait_recv()
        here = pl.ds(pl.multiple_of(t * ROWS + k * RW, RW), RW)
        for i, d in enumerate(tps):
            for j, (source, q) in enumerate(parts[i]):
                s3[k, i, :, j * Q : (j + 1) * Q] = r2[k][source, q]
            last.append(send(s3.at[k, i], o_ref.at[here], ss3.at[k, i], rs3.at[k, i], f, d))
        for j, (source, q) in enumerate(my_parts):
            o_ref[here, j * Q : (j + 1) * Q] = r2[k][source, q]
    for c in last:
        c.wait_recv()
    for c in spread + home + last:
        c.wait_send()


def backward(owner, scaled):
    n_t, n_f = len(T_STEPS), len(F_STEPS)
    return pl.pallas_call(
        backward_kernel,
        out_shape=jax.ShapeDtypeStruct((N_T * ROWS, OUT_COLS), jnp.bfloat16),
        in_specs=[pl.BlockSpec(memory_space=pltpu.SMEM), pl.BlockSpec(memory_space=VMEM)],
        out_specs=pl.BlockSpec(memory_space=VMEM),
        scratch_shapes=[VMEM((N_T, 2, RW, BLOCK), jnp.bfloat16)] * CHUNKS
        + [VMEM((CHUNKS, n_f, BLOCK // Q, RW, Q), jnp.bfloat16)]
        + [VMEM((N_F, BLOCK // Q, RW, Q), jnp.bfloat16)] * CHUNKS
        + [VMEM((CHUNKS, n_t, RW, OUT_COLS), jnp.bfloat16)]
        + [DMA((CHUNKS, n_t))] * 2
        + [DMA((CHUNKS, n_f))] * 2
        + [DMA((CHUNKS, n_t))] * 2,
        compiler_params=pltpu.CompilerParams(collective_id=1, has_side_effects=True, vmem_limit_bytes=32 << 20),
        name="backward",
    )(owner, scaled)


def per_device(gradient, owner, l_stat, r_stat, l_root, r_root):
    g = forward(owner, gradient)
    scaled = roots(g, l_root[0], r_root[0])
    update = backward(owner, scaled)
    new_left, new_right = stats(owner, g, l_stat[0], r_stat[0])
    return (update, new_left[None], new_right[None])


def solution(mesh):
    stat = P(("fsdp", "tp"), None, None)
    return jax.shard_map(
        per_device,
        mesh=mesh,
        in_specs=(P(("fsdp", "tp"), None), P(), stat, stat, stat, stat),
        out_specs=(P("fsdp", "tp"), stat, stat),
        check_vma=False,
    )
```

```python
import jax
import jax.numpy as jnp
from jax import lax
from jax.experimental import pallas as pl
from jax.experimental.pallas import tpu as pltpu
from jax.sharding import PartitionSpec as P

MESH = pl.DeviceIdType.MESH
VMEM = pltpu.VMEM
DMA = pltpu.SemaphoreType.DMA
f32, bf16 = jnp.float32, jnp.bfloat16

decay = 0.9
eps = 1e-06

BLOCK = 1024
LINES = 8
COLS = 10
N_F = 16
N_T = 8
RING = 4
ROWS = 64
CW = 128
FWD = BLOCK // CW
PAIR = 256
RW = 16
GROUPS = ROWS // RW
HW = 512
HALVES = BLOCK // HW
BWD = GROUPS * HALVES
OUT_COLS = 1280
Q = 256
QH = HW // Q
TILE = 256

F_STEPS = [(2, 2), (1, 2), (2, 1), (3, 2), (2, 3), (1, 1), (3, 3), (1, 3), (3, 1), (0, 2), (2, 0), (0, 1), (1, 0), (0, 3), (3, 0)]
T_STEPS = [(2, 0), (2, 1), (1, 0), (3, 0), (1, 1), (3, 1), (0, 1)]
NF, NT = len(F_STEPS), len(T_STEPS)


def fsdp_at(f, step):
    y = (f // RING + step[0]) % RING
    x = (f % RING + step[1]) % RING
    return y * RING + x


def tp_at(t, step):
    return ((t // 2 + step[0]) % RING) * 2 + (t % 2 + step[1]) % 2


def send(src, dst, send_sem, recv_sem, f, t):
    pltpu.make_async_remote_copy(
        src_ref=src, dst_ref=dst, send_sem=send_sem, recv_sem=recv_sem, device_id=(f, t), device_id_type=MESH
    ).start()


def drain(like, sem):
    pltpu.make_async_copy(like, like, sem).wait()


def rows_of(ref, i):
    return ref[i // 2, pl.ds((i % 2) * 4, 4)].reshape(TILE, ref.shape[-1])


def kernel(owner_ref, g_hbm, ls_hbm, rs_hbm, lr_hbm, rr_hbm, upd, nl, nr, *scratch):
    (gv, lr, rr, g, gt, full, s, s1, s2, b2, b3, slots) = scratch[:12]
    r1 = scratch[12 : 12 + FWD]
    ra = scratch[12 + FWD : 12 + FWD + BWD]
    rx = scratch[12 + FWD + BWD : 12 + FWD + BWD + GROUPS]
    (gsem, lsem, ss1, rs1, ss2, rs2, sa, ra_sem, sx, rx_sem, sz, rz_sem) = scratch[12 + FWD + BWD + GROUPS :]

    f, t = lax.axis_index("fsdp"), lax.axis_index("tp")
    line, part = f // 2, f % 2
    fs = [fsdp_at(f, step) for step in F_STEPS]
    ts = [tp_at(t, step) for step in T_STEPS]

    loads = [pltpu.make_async_copy(g_hbm.at[:, c * BLOCK : (c + 1) * BLOCK], gv.at[c], gsem.at[c]) for c in range(COLS)]
    big = [
        pltpu.make_async_copy(lr_hbm, lr, lsem.at[0]),
        pltpu.make_async_copy(rr_hbm, rr, lsem.at[1]),
        pltpu.make_async_copy(ls_hbm, nl, lsem.at[2]),
        pltpu.make_async_copy(rs_hbm, nr, lsem.at[3]),
    ]
    for load in loads + big:
        load.start()

    barrier = pltpu.get_barrier_semaphore()
    for d in fs:
        pl.semaphore_signal(barrier, inc=1, device_id=(d, t), device_id_type=MESH)
    for d in ts:
        pl.semaphore_signal(barrier, inc=1, device_id=(f, d), device_id_type=MESH)

    near = [owner_ref[line * COLS + c] >> 3 for c in range(COLS)]

    def column_of(fsdp):
        col = jnp.int32(0)
        for c in range(COLS):
            col = jnp.where(near[c] == fsdp, c, col)
        return col

    cols = [column_of(d) for d in fs]
    my_col = column_of(f)
    pl.semaphore_wait(barrier, NF + NT)
    for load in loads:
        load.wait()

    for k in range(FWD):
        cut = slice(k * CW, (k + 1) * CW)
        for i, d in enumerate(fs):
            s1[k, i] = gv[cols[i], :, cut]
            send(s1.at[k, i], r1[k].at[line, part], ss1.at[k], rs1.at[k], d, t)
        r1[k][line, part] = gv[my_col, :, cut]

    owned = [jnp.int32(-1)] * N_T
    for r in range(LINES):
        tp = jnp.int32(0)
        for c in range(COLS):
            o = owner_ref[r * COLS + c]
            here = (o >> 3) == f
            low = o & 7
            tp = jnp.where(here, low, tp)
            away = jnp.where(here, low, -1)
            owned = [jnp.where(away == p, r, owned[p]) for p in range(N_T)]
        slots[N_T + r] = tp
    for p in range(N_T):
        slots[p] = owned[p]
    mine = slots[t]
    has = mine >= 0
    lines = [jnp.maximum(slots[d], 0) for d in ts]
    my_line = jnp.maximum(mine, 0)

    def products(m, total):
        pair = slice(m * PAIR, (m + 1) * PAIR)
        drain(s2.at[2 * m], rs2.at[2 * m])
        drain(s2.at[2 * m + 1], rs2.at[2 * m + 1])
        block = g[:, :, :, pair].reshape(BLOCK, PAIR)

        def step(i, total):
            rows = pl.ds(pl.multiple_of(i * TILE, TILE), TILE)
            h = jnp.dot(lr[rows], block, preferred_element_type=f32).astype(bf16)
            for j in range(BLOCK // TILE):
                cut = slice(j * TILE, (j + 1) * TILE)
                p = jnp.dot(h, rr[pair, cut], preferred_element_type=f32)
                if m:
                    p += full[rows, cut]
                full[rows, cut] = p
                if m == BLOCK // PAIR - 1:
                    total += jnp.sum((p * p).reshape(TILE // 8, 8, TILE), axis=0)
            return total

        total = lax.fori_loop(0, BLOCK // TILE, step, total)
        gt[pair, :] = block.T
        return total

    total = jnp.zeros((8, TILE), f32)
    for k in range(FWD):
        drain(s1.at[k], rs1.at[k])
        cut = slice(k * CW, (k + 1) * CW)
        for i, d in enumerate(ts):
            s2[k, i] = r1[k][lines[i]]
            send(s2.at[k, i], g.at[:, t, :, cut], ss2.at[k], rs2.at[k], f, d)
        g[:, t, :, cut] = r1[k][my_line]
        if k == 3:
            for load in big[:2]:
                load.wait()
            total = products(0, total)
        elif k in (5, 7):
            total = products((k - 3) // 2, total)
    total = products(BLOCK // PAIR - 1, total)
    factor = lax.rsqrt(jnp.sum(total) / (BLOCK * BLOCK) + eps)

    for r in range(GROUPS):
        for h in range(2):
            for p in range(N_T):
                start = h * (BLOCK // 2) + p * ROWS + r * RW
                s[h, p, r * RW : (r + 1) * RW] = (full[start : start + RW] * factor).astype(bf16)
        rows = pl.ds(r * RW, RW)
        for e in range(HALVES):
            c = r * HALVES + e
            cut = pl.ds(e * HW, HW)
            for i, d in enumerate(ts):
                send(s.at[:, d, rows, cut], ra[c].at[t], sa.at[c], ra_sem.at[c], f, d)
            ra[c][t] = s[:, t, rows, cut]

    def left(i):
        rows = pl.ds(i * TILE, TILE)
        a = rows_of(g, i)
        for j in range(BLOCK // TILE):
            cut = slice(j * TILE, (j + 1) * TILE)
            p = jnp.dot(a, gt[:, cut], preferred_element_type=f32)
            nl[rows, cut] = decay * nl[rows, cut] + jnp.where(has, (1.0 - decay) * p, 0.0)

    def right(i):
        rows = pl.ds(i * TILE, TILE)
        a = gt[rows]
        for j in range(BLOCK // TILE):
            cut = slice(j * TILE, (j + 1) * TILE)
            p = jnp.dot(a, g[:, :, :, cut].reshape(BLOCK, TILE), preferred_element_type=f32)
            nr[rows, cut] = decay * nr[rows, cut] + jnp.where(has, (1.0 - decay) * p, 0.0)

    for load in big[2:]:
        load.wait()
    work = [lambda i=i: left(i) for i in range(4)] + [lambda i=i: right(i) for i in range(4)]
    work.pop(0)()
    work.pop(0)()

    def parts_of(tp):
        parts = []
        for j in range(OUT_COLS // Q):
            chunk = tp * (OUT_COLS // Q) + j
            parts.append((owner_ref[line * COLS + chunk // (BLOCK // Q)] >> 3, chunk % (BLOCK // Q)))
        return parts

    sources = [slots[N_T + d // 2] for d in fs]
    my_source = slots[N_T + line]
    parts = [parts_of(d) for d in ts]
    my_parts = parts_of(t)

    def finish(r):
        for e in range(HALVES):
            drain(b2.at[r * HALVES + e], rx_sem.at[r * HALVES + e])
        here = pl.ds(pl.multiple_of(t * ROWS + r * RW, RW), RW)
        for i, d in enumerate(ts):
            for j, (source, q) in enumerate(parts[i]):
                b3[r, i, :, j * Q : (j + 1) * Q] = rx[r][source, q]
            send(b3.at[r, i], upd.at[here], sz.at[r], rz_sem.at[r], f, d)
        for j, (source, q) in enumerate(my_parts):
            upd[here, j * Q : (j + 1) * Q] = rx[r][source, q]

    for c in range(BWD):
        r, e = c // HALVES, c % HALVES
        drain(ra[c].at[pl.ds(0, NT)], ra_sem.at[c])
        for i, d in enumerate(fs):
            piece = ra[c][sources[i], d % 2]
            for q in range(QH):
                b2[c, i, q] = piece[:, q * Q : (q + 1) * Q]
            send(b2.at[c, i], rx[r].at[f, pl.ds(e * QH, QH)], sx.at[c], rx_sem.at[c], d, t)
        piece = ra[c][my_source, part]
        for q in range(QH):
            rx[r][f, e * QH + q] = piece[:, q * Q : (q + 1) * Q]
        if e == HALVES - 1 and r > 0:
            finish(r - 1)
        if work:
            work.pop(0)()
    finish(GROUPS - 1)

    for k in range(FWD):
        drain(s1.at[k], ss1.at[k])
        drain(s2.at[k], ss2.at[k])
    for c in range(BWD):
        drain(ra[c].at[pl.ds(0, NT)], sa.at[c])
        drain(b2.at[c], sx.at[c])
    for r in range(GROUPS):
        drain(b3.at[r], sz.at[r])
        drain(b3.at[r], rz_sem.at[r])


def step(owner, gradient, l_stat, r_stat, l_root, r_root):
    hbm = pl.BlockSpec(memory_space=pltpu.HBM)
    vmem = pl.BlockSpec(memory_space=VMEM)
    return pl.pallas_call(
        kernel,
        out_shape=[
            VMEM((N_T * ROWS, OUT_COLS), bf16),
            VMEM((BLOCK, BLOCK), f32),
            VMEM((BLOCK, BLOCK), f32),
        ],
        in_specs=[pl.BlockSpec(memory_space=pltpu.SMEM)] + [hbm] * 5,
        out_specs=[vmem] * 3,
        scratch_shapes=[
            VMEM((COLS, ROWS, BLOCK), bf16),
            VMEM((BLOCK, BLOCK), bf16),
            VMEM((BLOCK, BLOCK), bf16),
            VMEM((2, N_T, ROWS, BLOCK), bf16),
            VMEM((BLOCK, BLOCK), bf16),
            VMEM((BLOCK, BLOCK), f32),
            VMEM((2, N_T, ROWS, BLOCK), bf16),
            VMEM((FWD, NF, ROWS, CW), bf16),
            VMEM((FWD, NT, 2, ROWS, CW), bf16),
            VMEM((BWD, NF, QH, RW, Q), bf16),
            VMEM((GROUPS, NT, RW, OUT_COLS), bf16),
            pltpu.SMEM((N_T + LINES,), jnp.int32),
        ]
        + [VMEM((LINES, 2, ROWS, CW), bf16)] * FWD
        + [VMEM((N_T, 2, RW, HW), bf16)] * BWD
        + [VMEM((N_F, BLOCK // Q, RW, Q), bf16)] * GROUPS
        + [DMA((COLS,)), DMA((4,))]
        + [DMA((FWD,))] * 4
        + [DMA((BWD,))] * 4
        + [DMA((GROUPS,))] * 2,
        compiler_params=pltpu.CompilerParams(collective_id=0, has_side_effects=True, vmem_limit_bytes=40 << 20),
        name="shampoo",
    )(owner, gradient, l_stat, r_stat, l_root, r_root)


def write_kernel(a, b, c, oa, ob, oc, sems):
    copies = [pltpu.make_async_copy(x, y, sems.at[i]) for i, (x, y) in enumerate([(a, oa), (b, ob), (c, oc)])]
    for copy in copies:
        copy.start()
    for copy in copies:
        copy.wait()


def write(update, new_left, new_right):
    outs = (update, new_left, new_right)
    return pl.pallas_call(
        write_kernel,
        out_shape=[jax.ShapeDtypeStruct(x.shape, x.dtype) for x in outs],
        in_specs=[pl.BlockSpec(memory_space=VMEM)] * 3,
        out_specs=[pl.BlockSpec(memory_space=pltpu.HBM)] * 3,
        scratch_shapes=[DMA((3,))],
        compiler_params=pltpu.CompilerParams(vmem_limit_bytes=16 << 20),
        name="write",
    )(*outs)


def per_device(gradient, owner, l_stat, r_stat, l_root, r_root):
    args = [pltpu.with_memory_space_constraint(x, pltpu.HBM) for x in (gradient, l_stat[0], r_stat[0], l_root[0], r_root[0])]
    update, new_left, new_right = write(*step(owner, *args))
    return (update, new_left[None], new_right[None])


def solution(mesh):
    stat = P(("fsdp", "tp"), None, None)
    return jax.shard_map(
        per_device,
        mesh=mesh,
        in_specs=(P(("fsdp", "tp"), None), P(), stat, stat, stat, stat),
        out_specs=(P("fsdp", "tp"), stat, stat),
        check_vma=False,
    )
```

```python
import jax
import jax.numpy as jnp
from jax import lax
from jax.experimental import pallas as pl
from jax.experimental.pallas import tpu as pltpu
from jax.sharding import PartitionSpec as P

MESH = pl.DeviceIdType.MESH
VMEM = pltpu.VMEM
DMA = pltpu.SemaphoreType.DMA
f32, bf16 = jnp.float32, jnp.bfloat16

decay = 0.9
eps = 1e-06

BLOCK = 1024
LINES = 8
COLS = 10
N_F = 16
N_T = 8
RING = 4
ROWS = 64
CW = 128
CHUNKS = [(0, 0, 32), (0, 32, 32)]
CHUNKS += [(c, 0, 64) for c in range(CW, BLOCK - CW, CW)]
CHUNKS += [(BLOCK - CW, 0, 32), (BLOCK - CW, 32, 32)]
FWD = len(CHUNKS)
PAIR = 256
RW = 16
GROUPS = ROWS // RW
HW = 512
HALVES = BLOCK // HW
BWD = GROUPS * HALVES
OUT_COLS = 1280
Q = 256
QH = HW // Q
TILE = 256

F_STEPS = [(2, 2), (1, 2), (2, 1), (3, 2), (2, 3), (1, 1), (3, 3), (1, 3), (3, 1), (0, 2), (2, 0), (0, 1), (1, 0), (0, 3), (3, 0)]
T_STEPS = [(2, 0), (2, 1), (1, 0), (3, 0), (1, 1), (3, 1), (0, 1)]
NF, NT = len(F_STEPS), len(T_STEPS)


def fsdp_at(f, step):
    y = (f // RING + step[0]) % RING
    x = (f % RING + step[1]) % RING
    return y * RING + x


def tp_at(t, step):
    return ((t // 2 + step[0]) % RING) * 2 + (t % 2 + step[1]) % 2


def send(src, dst, send_sem, recv_sem, f, t):
    pltpu.make_async_remote_copy(
        src_ref=src, dst_ref=dst, send_sem=send_sem, recv_sem=recv_sem, device_id=(f, t), device_id_type=MESH
    ).start()


def drain(like, sem):
    pltpu.make_async_copy(like, like, sem).wait()


def rows_of(ref, i):
    return ref[i // 2, pl.ds((i % 2) * 4, 4)].reshape(TILE, ref.shape[-1])


def kernel(owner_hbm, g_hbm, ls_hbm, rs_hbm, lr_hbm, rr_hbm, upd, nl, nr, *scratch):
    scratch = list(scratch)

    def take(n):
        taken, scratch[:n] = scratch[:n], []
        return taken

    gv, lr, rr, g, gt, full, s, b2, b3, owner_ref, slots = take(11)
    s1, s2, r1, ra, rx = take(FWD), take(FWD), take(FWD), take(BWD), take(GROUPS)
    gsem, lsem, ss1, rs1, ss2, rs2, sa, ra_sem, sx, rx_sem, sz, rz_sem = scratch

    f, t = lax.axis_index("fsdp"), lax.axis_index("tp")
    line, part = f // 2, f % 2
    fs = [fsdp_at(f, step) for step in F_STEPS]
    ts = [tp_at(t, step) for step in T_STEPS]

    barrier = pltpu.get_barrier_semaphore()
    for d in fs:
        pl.semaphore_signal(barrier, inc=1, device_id=(d, t), device_id_type=MESH)
    for d in ts:
        pl.semaphore_signal(barrier, inc=1, device_id=(f, d), device_id_type=MESH)

    names = pltpu.make_async_copy(owner_hbm, owner_ref, lsem.at[4])
    names.start()
    loads = [pltpu.make_async_copy(g_hbm.at[:, c * BLOCK : (c + 1) * BLOCK], gv.at[c], gsem.at[c]) for c in range(COLS)]
    big = [
        pltpu.make_async_copy(lr_hbm, lr, lsem.at[0]),
        pltpu.make_async_copy(rr_hbm, rr, lsem.at[1]),
        pltpu.make_async_copy(ls_hbm, nl, lsem.at[2]),
        pltpu.make_async_copy(rs_hbm, nr, lsem.at[3]),
    ]
    for load in loads:
        load.start()
    names.wait()

    near = [owner_ref[line * COLS + c] >> 3 for c in range(COLS)]

    def column_of(fsdp):
        col = jnp.int32(0)
        for c in range(COLS):
            col = jnp.where(near[c] == fsdp, c, col)
        return col

    cols = [column_of(d) for d in fs]
    my_col = column_of(f)
    pl.semaphore_wait(barrier, NF + NT)
    for load in loads:
        load.wait()

    for k, (c0, r0, n) in enumerate(CHUNKS):
        for i, d in enumerate(fs):
            s1[k][i] = gv[cols[i], r0 : r0 + n, c0 : c0 + CW]
            send(s1[k].at[i], r1[k].at[line, part], ss1.at[k], rs1.at[k], d, t)
        r1[k][line, part] = gv[my_col, r0 : r0 + n, c0 : c0 + CW]
        if k == 1:
            for load in big:
                load.start()

    owned = [jnp.int32(-1)] * N_T
    for r in range(LINES):
        tp = jnp.int32(0)
        for c in range(COLS):
            o = owner_ref[r * COLS + c]
            here = (o >> 3) == f
            low = o & 7
            tp = jnp.where(here, low, tp)
            away = jnp.where(here, low, -1)
            owned = [jnp.where(away == p, r, owned[p]) for p in range(N_T)]
        slots[N_T + r] = tp
    for p in range(N_T):
        slots[p] = owned[p]
    mine = slots[t]
    has = mine >= 0
    lines = [jnp.maximum(slots[d], 0) for d in ts]
    my_line = jnp.maximum(mine, 0)

    def turn(m):
        pair = slice(m * PAIR, (m + 1) * PAIR)
        gt[pair, :] = g[:, :, :, pair].reshape(BLOCK, PAIR).T

    def products(m):
        pair = slice(m * PAIR, (m + 1) * PAIR)
        for k, (c0, _, _) in enumerate(CHUNKS):
            if c0 // PAIR == m:
                drain(s2[k], rs2.at[k])
        h = jnp.dot(lr[...], g[:, :, :, pair].reshape(BLOCK, PAIR), preferred_element_type=f32).astype(bf16)
        total = jnp.zeros((8, TILE), f32)
        for i in range(BLOCK // TILE):
            rows = slice(i * TILE, (i + 1) * TILE)
            for j in range(BLOCK // TILE):
                cut = slice(j * TILE, (j + 1) * TILE)
                p = jnp.dot(h[rows], rr[pair, cut], preferred_element_type=f32)
                if m:
                    p += full[rows, cut]
                full[rows, cut] = p
                total += jnp.sum((p * p).reshape(TILE // 8, 8, TILE), axis=0)
        return total

    for k, (c0, r0, n) in enumerate(CHUNKS):
        drain(s1[k], rs1.at[k])
        for i, d in enumerate(ts):
            s2[k][i] = r1[k][lines[i]]
            send(s2[k].at[i], g.at[:, t, pl.ds(r0, n), c0 : c0 + CW], ss2.at[k], rs2.at[k], f, d)
        g[:, t, r0 : r0 + n, c0 : c0 + CW] = r1[k][my_line]
        if k == 4:
            for load in big[:2]:
                load.wait()
        if k in (5, 7, 9):
            products((k - 5) // 2)
            turn((k - 5) // 2)
    total = products(BLOCK // PAIR - 1)
    factor = lax.rsqrt(jnp.sum(total) / (BLOCK * BLOCK) + eps)

    for r in range(GROUPS):
        for h in range(2):
            for p in range(N_T):
                start = h * (BLOCK // 2) + p * ROWS + r * RW
                s[h, p, r * RW : (r + 1) * RW] = (full[start : start + RW] * factor).astype(bf16)
        rows = pl.ds(r * RW, RW)
        for e in range(HALVES):
            c = r * HALVES + e
            cut = pl.ds(e * HW, HW)
            for i, d in enumerate(ts):
                send(s.at[:, d, rows, cut], ra[c].at[t], sa.at[c], ra_sem.at[c], f, d)
            ra[c][t] = s[:, t, rows, cut]

    def left(i):
        rows = pl.ds(i * TILE, TILE)
        a = rows_of(g, i)
        for j in range(BLOCK // TILE):
            cut = slice(j * TILE, (j + 1) * TILE)
            p = jnp.dot(a, gt[:, cut], preferred_element_type=f32)
            nl[rows, cut] = decay * nl[rows, cut] + jnp.where(has, (1.0 - decay) * p, 0.0)

    def right(i):
        rows = pl.ds(i * TILE, TILE)
        a = gt[rows]
        for j in range(BLOCK // TILE):
            cut = slice(j * TILE, (j + 1) * TILE)
            p = jnp.dot(a, g[:, :, :, cut].reshape(BLOCK, TILE), preferred_element_type=f32)
            nr[rows, cut] = decay * nr[rows, cut] + jnp.where(has, (1.0 - decay) * p, 0.0)

    turn(BLOCK // PAIR - 1)
    for load in big[2:]:
        load.wait()
    work = [lambda i=i: left(i) for i in range(4)] + [lambda i=i: right(i) for i in range(4)]
    work.pop(0)()
    work.pop(0)()

    def parts_of(tp):
        parts = []
        for j in range(OUT_COLS // Q):
            chunk = tp * (OUT_COLS // Q) + j
            parts.append((owner_ref[line * COLS + chunk // (BLOCK // Q)] >> 3, chunk % (BLOCK // Q)))
        return parts

    sources = [slots[N_T + d // 2] for d in fs]
    my_source = slots[N_T + line]
    parts = [parts_of(d) for d in ts]
    my_parts = parts_of(t)

    def finish(r):
        for e in range(HALVES):
            drain(b2.at[r * HALVES + e], rx_sem.at[r * HALVES + e])
        here = pl.ds(pl.multiple_of(t * ROWS + r * RW, RW), RW)
        for i, d in enumerate(ts):
            for j, (source, q) in enumerate(parts[i]):
                b3[r, i, :, j * Q : (j + 1) * Q] = rx[r][source, q]
            send(b3.at[r, i], upd.at[here], sz.at[r], rz_sem.at[r], f, d)
        for j, (source, q) in enumerate(my_parts):
            upd[here, j * Q : (j + 1) * Q] = rx[r][source, q]

    for c in range(BWD):
        r, e = c // HALVES, c % HALVES
        drain(ra[c].at[pl.ds(0, NT)], ra_sem.at[c])
        for i, d in enumerate(fs):
            piece = ra[c][sources[i], d % 2]
            for q in range(QH):
                b2[c, i, q] = piece[:, q * Q : (q + 1) * Q]
            send(b2.at[c, i], rx[r].at[f, pl.ds(e * QH, QH)], sx.at[c], rx_sem.at[c], d, t)
        piece = ra[c][my_source, part]
        for q in range(QH):
            rx[r][f, e * QH + q] = piece[:, q * Q : (q + 1) * Q]
        if e == HALVES - 1 and r > 0:
            finish(r - 1)
        if work:
            work.pop(0)()
    finish(GROUPS - 1)

    for k in range(FWD):
        drain(s1[k], ss1.at[k])
        drain(s2[k], ss2.at[k])
    for c in range(BWD):
        drain(ra[c].at[pl.ds(0, NT)], sa.at[c])
        drain(b2.at[c], sx.at[c])
    for r in range(GROUPS):
        drain(b3.at[r], sz.at[r])
        drain(b3.at[r], rz_sem.at[r])


def step(owner, gradient, l_stat, r_stat, l_root, r_root):
    hbm = pl.BlockSpec(memory_space=pltpu.HBM)
    vmem = pl.BlockSpec(memory_space=VMEM)
    return pl.pallas_call(
        kernel,
        out_shape=[
            VMEM((N_T * ROWS, OUT_COLS), bf16),
            VMEM((BLOCK, BLOCK), f32),
            VMEM((BLOCK, BLOCK), f32),
        ],
        in_specs=[hbm] * 6,
        out_specs=[vmem] * 3,
        scratch_shapes=[
            VMEM((COLS, ROWS, BLOCK), bf16),
            VMEM((BLOCK, BLOCK), bf16),
            VMEM((BLOCK, BLOCK), bf16),
            VMEM((2, N_T, ROWS, BLOCK), bf16),
            VMEM((BLOCK, BLOCK), bf16),
            VMEM((BLOCK, BLOCK), f32),
            VMEM((2, N_T, ROWS, BLOCK), bf16),
            VMEM((BWD, NF, QH, RW, Q), bf16),
            VMEM((GROUPS, NT, RW, OUT_COLS), bf16),
            pltpu.SMEM((LINES * COLS,), jnp.int32),
            pltpu.SMEM((N_T + LINES,), jnp.int32),
        ]
        + [VMEM((NF, n, CW), bf16) for _, _, n in CHUNKS]
        + [VMEM((NT, 2, n, CW), bf16) for _, _, n in CHUNKS]
        + [VMEM((LINES, 2, n, CW), bf16) for _, _, n in CHUNKS]
        + [VMEM((N_T, 2, RW, HW), bf16)] * BWD
        + [VMEM((N_F, BLOCK // Q, RW, Q), bf16)] * GROUPS
        + [DMA((COLS,)), DMA((5,))]
        + [DMA((FWD,))] * 4
        + [DMA((BWD,))] * 4
        + [DMA((GROUPS,))] * 2,
        compiler_params=pltpu.CompilerParams(collective_id=0, has_side_effects=True, vmem_limit_bytes=40 << 20),
        name="shampoo",
    )(owner, gradient, l_stat, r_stat, l_root, r_root)


def write_kernel(a, b, c, oa, ob, oc, sems):
    copies = [pltpu.make_async_copy(x, y, sems.at[i]) for i, (x, y) in enumerate([(a, oa), (b, ob), (c, oc)])]
    for copy in copies:
        copy.start()
    for copy in copies:
        copy.wait()


def write(update, new_left, new_right):
    outs = (update, new_left, new_right)
    return pl.pallas_call(
        write_kernel,
        out_shape=[jax.ShapeDtypeStruct(x.shape, x.dtype) for x in outs],
        in_specs=[pl.BlockSpec(memory_space=VMEM)] * 3,
        out_specs=[pl.BlockSpec(memory_space=pltpu.HBM)] * 3,
        scratch_shapes=[DMA((3,))],
        compiler_params=pltpu.CompilerParams(vmem_limit_bytes=16 << 20),
        name="write",
    )(*outs)


def per_device(gradient, owner, l_stat, r_stat, l_root, r_root):
    args = [pltpu.with_memory_space_constraint(x, pltpu.HBM) for x in (owner, gradient, l_stat[0], r_stat[0], l_root[0], r_root[0])]
    update, new_left, new_right = write(*step(*args))
    return (update, new_left[None], new_right[None])


def solution(mesh):
    stat = P(("fsdp", "tp"), None, None)
    return jax.shard_map(
        per_device,
        mesh=mesh,
        in_specs=(P(("fsdp", "tp"), None), P(), stat, stat, stat, stat),
        out_specs=(P("fsdp", "tp"), stat, stat),
        check_vma=False,
    )
```

```python
import jax
import jax.numpy as jnp
from jax import lax
from jax.experimental import pallas as pl
from jax.experimental.pallas import tpu as pltpu
from jax.sharding import PartitionSpec as P

MESH = pl.DeviceIdType.MESH
VMEM = pltpu.VMEM
DMA = pltpu.SemaphoreType.DMA
f32, bf16 = jnp.float32, jnp.bfloat16

decay = 0.9
eps = 1e-06

BLOCK = 1024
LINES = 8
COLS = 10
N_F = 16
N_T = 8
RING = 4
ROWS = 64
CW = 128
CHUNKS = [(0, 0, 32), (0, 32, 32)]
CHUNKS += [(c, 0, 64) for c in range(CW, BLOCK - CW, CW)]
CHUNKS += [(BLOCK - CW, 0, 32), (BLOCK - CW, 32, 32)]
FWD = len(CHUNKS)
PAIR = 256
RW = 16
GROUPS = ROWS // RW
OUT_COLS = 1280
Q = 256
TILE = 256
BACK = [(0, 0, 512), (0, 512, 512)] + [(r, c, 512) for r in range(1, GROUPS) for c in (0, 512)]
BWD = len(BACK)

F_STEPS = [(2, 2), (1, 2), (2, 1), (3, 2), (2, 3), (1, 1), (3, 3), (1, 3), (3, 1), (0, 2), (2, 0), (0, 1), (1, 0), (0, 3), (3, 0)]
T_STEPS = [(2, 0), (2, 1), (1, 0), (3, 0), (1, 1), (3, 1), (0, 1)]
NF, NT = len(F_STEPS), len(T_STEPS)


def fsdp_at(f, step):
    y = (f // RING + step[0]) % RING
    x = (f % RING + step[1]) % RING
    return y * RING + x


def tp_at(t, step):
    return ((t // 2 + step[0]) % RING) * 2 + (t % 2 + step[1]) % 2


def send(src, dst, send_sem, recv_sem, f, t):
    pltpu.make_async_remote_copy(
        src_ref=src, dst_ref=dst, send_sem=send_sem, recv_sem=recv_sem, device_id=(f, t), device_id_type=MESH
    ).start()


def drain(like, sem):
    pltpu.make_async_copy(like, like, sem).wait()


def rows_of(ref, i):
    return ref[i // 2, pl.ds((i % 2) * 4, 4)].reshape(TILE, ref.shape[-1])


def kernel(owner_hbm, g_hbm, ls_hbm, rs_hbm, lr_hbm, rr_hbm, upd, nl, nr, *scratch):
    scratch = list(scratch)

    def take(n):
        taken, scratch[:n] = scratch[:n], []
        return taken

    gv, lr, rr, g, gt, full, s, b3, fac, fac_out, owner_ref, slots = take(12)
    s1, s2, r1, ra, b2, rx = take(FWD), take(FWD), take(FWD), take(BWD), take(BWD), take(GROUPS)
    gsem, lsem, ss1, rs1, ss2, rs2, sa, ra_sem, sx, rx_sem, sz, rz_sem, sf, rf_sem = scratch

    f, t = lax.axis_index("fsdp"), lax.axis_index("tp")
    line, part = f // 2, f % 2
    fs = [fsdp_at(f, step) for step in F_STEPS]
    ts = [tp_at(t, step) for step in T_STEPS]

    barrier = pltpu.get_barrier_semaphore()
    for d in fs:
        pl.semaphore_signal(barrier, inc=1, device_id=(d, t), device_id_type=MESH)
    for d in ts:
        pl.semaphore_signal(barrier, inc=1, device_id=(f, d), device_id_type=MESH)

    names = pltpu.make_async_copy(owner_hbm, owner_ref, lsem.at[4])
    names.start()
    loads = [pltpu.make_async_copy(g_hbm.at[:, c * BLOCK : (c + 1) * BLOCK], gv.at[c], gsem.at[c]) for c in range(COLS)]
    big = [
        pltpu.make_async_copy(lr_hbm.at[:, :, r], lr.at[r], lsem.at[5 + r]) for r in range(GROUPS)
    ] + [
        pltpu.make_async_copy(rr_hbm, rr, lsem.at[1]),
        pltpu.make_async_copy(ls_hbm, nl, lsem.at[2]),
        pltpu.make_async_copy(rs_hbm, nr, lsem.at[3]),
    ]
    for load in loads:
        load.start()
    names.wait()

    near = [owner_ref[line * COLS + c] >> 3 for c in range(COLS)]

    def column_of(fsdp):
        col = jnp.int32(0)
        for c in range(COLS):
            col = jnp.where(near[c] == fsdp, c, col)
        return col

    cols = [column_of(d) for d in fs]
    my_col = column_of(f)
    pl.semaphore_wait(barrier, NF + NT)
    for load in loads:
        load.wait()

    for k, (c0, r0, n) in enumerate(CHUNKS):
        for i, d in enumerate(fs):
            s1[k][i] = gv[cols[i], r0 : r0 + n, c0 : c0 + CW]
            send(s1[k].at[i], r1[k].at[line, part], ss1.at[k], rs1.at[k], d, t)
        r1[k][line, part] = gv[my_col, r0 : r0 + n, c0 : c0 + CW]
        if k == 1:
            for load in big:
                load.start()

    owned = [jnp.int32(-1)] * N_T
    for r in range(LINES):
        tp = jnp.int32(0)
        for c in range(COLS):
            o = owner_ref[r * COLS + c]
            here = (o >> 3) == f
            low = o & 7
            tp = jnp.where(here, low, tp)
            away = jnp.where(here, low, -1)
            owned = [jnp.where(away == p, r, owned[p]) for p in range(N_T)]
        slots[N_T + r] = tp
    for p in range(N_T):
        slots[p] = owned[p]
    mine = slots[t]
    has = mine >= 0
    lines = [jnp.maximum(slots[d], 0) for d in ts]
    my_line = jnp.maximum(mine, 0)

    def cut_rows(r, factor):
        for h in range(2):
            for p in range(N_T):
                start = r * TILE + (h * N_T + p) * RW
                rows = full[start : start + RW]
                s[h, p, r * RW : (r + 1) * RW] = (rows if factor is None else rows * factor).astype(bf16)

    def spread(c):
        r, c0, width = BACK[c]
        rows, cut = pl.ds(r * RW, RW), pl.ds(c0, width)
        for i, d in enumerate(ts):
            send(s.at[:, d, rows, cut], ra[c].at[t], sa.at[c], ra_sem.at[c], f, d)
        ra[c][t] = s[:, t, rows, cut]

    def turn(m):
        pair = slice(m * PAIR, (m + 1) * PAIR)
        gt[pair, :] = g[:, :, :, pair].reshape(BLOCK, PAIR).T

    def products(m):
        pair = slice(m * PAIR, (m + 1) * PAIR)
        for k, (c0, _, _) in enumerate(CHUNKS):
            if c0 // PAIR == m:
                drain(s2[k], rs2.at[k])
        h = jnp.dot(lr[...].reshape(BLOCK, BLOCK), g[:, :, :, pair].reshape(BLOCK, PAIR), preferred_element_type=f32).astype(bf16)
        total = jnp.zeros((8, TILE), f32)
        for i in range(BLOCK // TILE):
            rows = slice(i * TILE, (i + 1) * TILE)
            for j in range(BLOCK // TILE):
                cut = slice(j * TILE, (j + 1) * TILE)
                p = jnp.dot(h[rows], rr[pair, cut], preferred_element_type=f32)
                if m:
                    p += full[rows, cut]
                full[rows, cut] = p
                if m == BLOCK // PAIR - 1:
                    total += jnp.sum((p * p).reshape(TILE // 8, 8, TILE), axis=0)
            if m == BLOCK // PAIR - 1 and i == 0:
                cut_rows(0, None)
                spread(0)
        return total

    for k, (c0, r0, n) in enumerate(CHUNKS):
        drain(s1[k], rs1.at[k])
        for i, d in enumerate(ts):
            s2[k][i] = r1[k][lines[i]]
            send(s2[k].at[i], g.at[:, t, pl.ds(r0, n), c0 : c0 + CW], ss2.at[k], rs2.at[k], f, d)
        g[:, t, r0 : r0 + n, c0 : c0 + CW] = r1[k][my_line]
        if k == 4:
            for load in big[:5]:
                load.wait()
        for m in range(BLOCK // PAIR - 1):
            if k == max(j for j in range(FWD) if CHUNKS[j][0] // PAIR == m) + 3:
                products(m)
                turn(m)
    total = products(BLOCK // PAIR - 1)
    factor = lax.rsqrt(jnp.sum(total, axis=(0, 1), keepdims=True) / (BLOCK * BLOCK) + eps)

    fac_out[...] = jnp.broadcast_to(factor, fac_out.shape)
    for d in ts:
        send(fac_out, fac.at[t], sf, rf_sem, f, d)
    fac[t] = jnp.broadcast_to(factor, fac_out.shape)
    for c in range(1, BWD):
        r, c0, _ = BACK[c]
        if r and not c0:
            cut_rows(r, factor)
        spread(c)

    def scaled(piece, slot, c):
        if BACK[c][0]:
            return piece
        scale = jnp.concatenate([fac[slot][0:1]] * (BACK[c][2] // 128), axis=1)
        return (piece.astype(f32) * scale).astype(bf16)


    def left(i):
        rows = pl.ds(i * TILE, TILE)
        a = rows_of(g, i)
        for j in range(BLOCK // TILE):
            cut = slice(j * TILE, (j + 1) * TILE)
            p = jnp.dot(a, gt[:, cut], preferred_element_type=f32)
            nl[rows, cut] = decay * nl[rows, cut] + jnp.where(has, (1.0 - decay) * p, 0.0)

    def right(i):
        rows = pl.ds(i * TILE, TILE)
        a = gt[rows]
        for j in range(BLOCK // TILE):
            cut = slice(j * TILE, (j + 1) * TILE)
            p = jnp.dot(a, g[:, :, :, cut].reshape(BLOCK, TILE), preferred_element_type=f32)
            nr[rows, cut] = decay * nr[rows, cut] + jnp.where(has, (1.0 - decay) * p, 0.0)

    turn(BLOCK // PAIR - 1)
    for load in big[5:]:
        load.wait()
    work = [lambda i=i: left(i) for i in range(4)] + [lambda i=i: right(i) for i in range(4)]
    work.pop(0)()
    work.pop(0)()

    def parts_of(tp):
        parts = []
        for j in range(OUT_COLS // Q):
            chunk = tp * (OUT_COLS // Q) + j
            parts.append((owner_ref[line * COLS + chunk // (BLOCK // Q)] >> 3, chunk % (BLOCK // Q)))
        return parts

    sources = [slots[N_T + d // 2] for d in fs]
    my_source = slots[N_T + line]
    parts = [parts_of(d) for d in ts]
    my_parts = parts_of(t)

    def finish(r):
        for c in range(BWD):
            if BACK[c][0] == r:
                drain(b2[c], rx_sem.at[c])
        here = pl.ds(pl.multiple_of(t * ROWS + r * RW, RW), RW)
        for i, d in enumerate(ts):
            for j, (source, q) in enumerate(parts[i]):
                b3[r, i, :, j * Q : (j + 1) * Q] = rx[r][source, q]
            send(b3.at[r, i], upd.at[here], sz.at[r], rz_sem.at[r], f, d)
        for j, (source, q) in enumerate(my_parts):
            upd[here, j * Q : (j + 1) * Q] = rx[r][source, q]

    for c, (r, c0, width) in enumerate(BACK):
        drain(ra[c].at[pl.ds(0, NT)], ra_sem.at[c])
        if c == 0:
            drain(fac.at[pl.ds(0, NT)], rf_sem)
        first, count = c0 // Q, width // Q
        for i, d in enumerate(fs):
            piece = scaled(ra[c][sources[i], d % 2], sources[i], c)
            for q in range(count):
                b2[c][i, q] = piece[:, q * Q : (q + 1) * Q]
            send(b2[c].at[i], rx[r].at[f, pl.ds(first, count)], sx.at[c], rx_sem.at[c], d, t)
        piece = scaled(ra[c][my_source, part], my_source, c)
        for q in range(count):
            rx[r][f, first + q] = piece[:, q * Q : (q + 1) * Q]
        if r and c0 + width == BLOCK:
            finish(r - 1)
        if work:
            work.pop(0)()
    finish(GROUPS - 1)

    for k in range(FWD):
        drain(s1[k], ss1.at[k])
        drain(s2[k], ss2.at[k])
    for c in range(BWD):
        drain(ra[c].at[pl.ds(0, NT)], sa.at[c])
        drain(b2[c], sx.at[c])
    drain(fac.at[pl.ds(0, NT)], sf)
    for r in range(GROUPS):
        drain(b3.at[r], sz.at[r])
        drain(b3.at[r], rz_sem.at[r])


def step(owner, gradient, l_stat, r_stat, l_root, r_root):
    hbm = pl.BlockSpec(memory_space=pltpu.HBM)
    vmem = pl.BlockSpec(memory_space=VMEM)
    return pl.pallas_call(
        kernel,
        out_shape=[
            VMEM((N_T * ROWS, OUT_COLS), bf16),
            VMEM((BLOCK, BLOCK), f32),
            VMEM((BLOCK, BLOCK), f32),
        ],
        in_specs=[hbm] * 6,
        out_specs=[vmem] * 3,
        scratch_shapes=[
            VMEM((COLS, ROWS, BLOCK), bf16),
            VMEM((GROUPS, 2, N_T, RW, BLOCK), bf16),
            VMEM((BLOCK, BLOCK), bf16),
            VMEM((2, N_T, ROWS, BLOCK), bf16),
            VMEM((BLOCK, BLOCK), bf16),
            VMEM((BLOCK, BLOCK), f32),
            VMEM((2, N_T, ROWS, BLOCK), bf16),
            VMEM((GROUPS, NT, RW, OUT_COLS), bf16),
            VMEM((N_T, 8, 128), f32),
            VMEM((8, 128), f32),
            pltpu.SMEM((LINES * COLS,), jnp.int32),
            pltpu.SMEM((N_T + LINES,), jnp.int32),
        ]
        + [VMEM((NF, n, CW), bf16) for _, _, n in CHUNKS]
        + [VMEM((NT, 2, n, CW), bf16) for _, _, n in CHUNKS]
        + [VMEM((LINES, 2, n, CW), bf16) for _, _, n in CHUNKS]
        + [VMEM((N_T, 2, RW, w), bf16) for _, _, w in BACK]
        + [VMEM((NF, w // Q, RW, Q), bf16) for _, _, w in BACK]
        + [VMEM((N_F, BLOCK // Q, RW, Q), bf16)] * GROUPS
        + [DMA((COLS,)), DMA((5 + GROUPS,))]
        + [DMA((FWD,))] * 4
        + [DMA((BWD,))] * 4
        + [DMA((GROUPS,))] * 2
        + [DMA] * 2,
        compiler_params=pltpu.CompilerParams(collective_id=0, has_side_effects=True, vmem_limit_bytes=40 << 20),
        name="shampoo",
    )(owner, gradient, l_stat, r_stat, l_root, r_root)


def write_kernel(a, b, c, oa, ob, oc, sems):
    copies = [pltpu.make_async_copy(x, y, sems.at[i]) for i, (x, y) in enumerate([(a, oa), (b, ob), (c, oc)])]
    for copy in copies:
        copy.start()
    for copy in copies:
        copy.wait()


def write(update, new_left, new_right):
    outs = (update, new_left, new_right)
    return pl.pallas_call(
        write_kernel,
        out_shape=[jax.ShapeDtypeStruct(x.shape, x.dtype) for x in outs],
        in_specs=[pl.BlockSpec(memory_space=VMEM)] * 3,
        out_specs=[pl.BlockSpec(memory_space=pltpu.HBM)] * 3,
        scratch_shapes=[DMA((3,))],
        compiler_params=pltpu.CompilerParams(vmem_limit_bytes=16 << 20),
        name="write",
    )(*outs)


def per_device(gradient, owner, l_stat, r_stat, l_root, r_root):
    args = (owner, gradient, l_stat[0], r_stat[0], l_root.reshape(2, N_T, GROUPS, RW, BLOCK), r_root[0])
    args = [pltpu.with_memory_space_constraint(x, pltpu.HBM) for x in args]
    update, new_left, new_right = write(*step(*args))
    return (update, new_left[None], new_right[None])


def solution(mesh):
    stat = P(("fsdp", "tp"), None, None)
    return jax.shard_map(
        per_device,
        mesh=mesh,
        in_specs=(P(("fsdp", "tp"), None), P(), stat, stat, stat, stat),
        out_specs=(P("fsdp", "tp"), stat, stat),
        check_vma=False,
    )
```

```python
import jax
import jax.numpy as jnp
from jax import lax
from jax.experimental import pallas as pl
from jax.experimental.pallas import tpu as pltpu
from jax.sharding import PartitionSpec as P

MESH = pl.DeviceIdType.MESH
VMEM = pltpu.VMEM
DMA = pltpu.SemaphoreType.DMA
f32, bf16 = jnp.float32, jnp.bfloat16

decay = 0.9
eps = 1e-06

BLOCK = 1024
LINES = 8
COLS = 10
N_F = 16
N_T = 8
RING = 4
ROWS = 64
CW = 128
CHUNKS = [(0, 0, 32), (0, 32, 32)]
CHUNKS += [(c, 0, 64) for c in range(CW, BLOCK - CW, CW)]
CHUNKS += [(BLOCK - CW, 0, 32), (BLOCK - CW, 32, 32)]
FWD = len(CHUNKS)
STAGED = 2
PAIR = 256
RW = 16
GROUPS = ROWS // RW
OUT_COLS = 1280
Q = 256
TILE = 256
BACK = [(0, 0, 512), (0, 512, 512)] + [(r, c, 512) for r in range(1, GROUPS) for c in (0, 512)]
BWD = len(BACK)

F_STEPS = [(2, 2), (1, 2), (2, 1), (3, 2), (2, 3), (1, 1), (3, 3), (1, 3), (3, 1), (0, 2), (2, 0), (0, 1), (1, 0), (0, 3), (3, 0)]
T_STEPS = [(2, 0), (2, 1), (1, 0), (3, 0), (1, 1), (3, 1), (0, 1)]
NF, NT = len(F_STEPS), len(T_STEPS)


def fsdp_at(f, step):
    y = (f // RING + step[0]) % RING
    x = (f % RING + step[1]) % RING
    return y * RING + x


def tp_at(t, step):
    return ((t // 2 + step[0]) % RING) * 2 + (t % 2 + step[1]) % 2


def send(src, dst, send_sem, recv_sem, f, t):
    pltpu.make_async_remote_copy(
        src_ref=src, dst_ref=dst, send_sem=send_sem, recv_sem=recv_sem, device_id=(f, t), device_id_type=MESH
    ).start()


def drain(like, sem):
    pltpu.make_async_copy(like, like, sem).wait()


def rows_of(ref, i):
    return ref[i // 2, pl.ds((i % 2) * 4, 4)].reshape(TILE, ref.shape[-1])


def kernel(owner_hbm, g_hbm, ls_hbm, rs_hbm, lr_hbm, rr_hbm, upd, nl, nr, *scratch):
    scratch = list(scratch)

    def take(n):
        taken, scratch[:n] = scratch[:n], []
        return taken

    gv, lr, rr, g, gt, full, s, b3, fac, fac_out, owner_ref, slots = take(12)
    s1, s2, r1, ra, b2, rx = take(FWD), take(FWD), take(FWD), take(BWD), take(BWD), take(GROUPS)
    gsem, lsem, ss1, rs1, ss2, rs2, sa, ra_sem, sx, rx_sem, sz, rz_sem, sf, rf_sem = scratch

    f, t = lax.axis_index("fsdp"), lax.axis_index("tp")
    line, part = f // 2, f % 2
    fs = [fsdp_at(f, step) for step in F_STEPS]
    ts = [tp_at(t, step) for step in T_STEPS]

    names = pltpu.make_async_copy(owner_hbm, owner_ref, lsem.at[4])
    names.start()
    barrier = pltpu.get_barrier_semaphore()
    for d in fs:
        pl.semaphore_signal(barrier, inc=1, device_id=(d, t), device_id_type=MESH)
    for d in ts:
        pl.semaphore_signal(barrier, inc=1, device_id=(f, d), device_id_type=MESH)

    loads = [pltpu.make_async_copy(g_hbm.at[:, c * BLOCK : (c + 1) * BLOCK], gv.at[c], gsem.at[c]) for c in range(COLS)]
    big = [
        pltpu.make_async_copy(lr_hbm.at[:, :, r], lr.at[r], lsem.at[5 + r]) for r in range(GROUPS)
    ] + [
        pltpu.make_async_copy(rr_hbm, rr, lsem.at[1]),
        pltpu.make_async_copy(ls_hbm, nl, lsem.at[2]),
        pltpu.make_async_copy(rs_hbm, nr, lsem.at[3]),
    ]
    for load in loads:
        load.start()
    names.wait()

    near = [owner_ref[line * COLS + c] >> 3 for c in range(COLS)]

    def column_of(fsdp):
        col = jnp.int32(0)
        for c in range(COLS):
            col = jnp.where(near[c] == fsdp, c, col)
        return col

    cols = [column_of(d) for d in fs]
    my_col = column_of(f)
    for load in loads:
        load.wait()

    def stage(k):
        c0, r0, n = CHUNKS[k]
        for i in range(NF):
            s1[k][i] = gv[cols[i], r0 : r0 + n, c0 : c0 + CW]
        r1[k][line, part] = gv[my_col, r0 : r0 + n, c0 : c0 + CW]

    for k in range(STAGED):
        stage(k)
    pl.semaphore_wait(barrier, NF + NT)
    for k in range(FWD):
        if k >= STAGED:
            stage(k)
        for i, d in enumerate(fs):
            send(s1[k].at[i], r1[k].at[line, part], ss1.at[k], rs1.at[k], d, t)
        if k == 1:
            for load in big:
                load.start()

    owned = [jnp.int32(-1)] * N_T
    for r in range(LINES):
        tp = jnp.int32(0)
        for c in range(COLS):
            o = owner_ref[r * COLS + c]
            here = (o >> 3) == f
            low = o & 7
            tp = jnp.where(here, low, tp)
            away = jnp.where(here, low, -1)
            owned = [jnp.where(away == p, r, owned[p]) for p in range(N_T)]
        slots[N_T + r] = tp
    for p in range(N_T):
        slots[p] = owned[p]
    mine = slots[t]
    has = mine >= 0
    lines = [jnp.maximum(slots[d], 0) for d in ts]
    my_line = jnp.maximum(mine, 0)

    def cut_rows(r, factor):
        for h in range(2):
            for p in range(N_T):
                start = r * TILE + (h * N_T + p) * RW
                rows = full[start : start + RW]
                s[h, p, r * RW : (r + 1) * RW] = (rows if factor is None else rows * factor).astype(bf16)

    def spread(c):
        r, c0, width = BACK[c]
        rows, cut = pl.ds(r * RW, RW), pl.ds(c0, width)
        for i, d in enumerate(ts):
            send(s.at[:, d, rows, cut], ra[c].at[t], sa.at[c], ra_sem.at[c], f, d)
        ra[c][t] = s[:, t, rows, cut]

    def turn(m):
        pair = slice(m * PAIR, (m + 1) * PAIR)
        gt[pair, :] = g[:, :, :, pair].reshape(BLOCK, PAIR).T

    def products(m):
        pair = slice(m * PAIR, (m + 1) * PAIR)
        for k, (c0, _, _) in enumerate(CHUNKS):
            if c0 // PAIR == m:
                drain(s2[k], rs2.at[k])
        block = g[:, :, :, pair].reshape(BLOCK, PAIR)
        final = m == BLOCK // PAIR - 1
        if not final:
            h = jnp.dot(lr[...].reshape(BLOCK, BLOCK), block, preferred_element_type=f32).astype(bf16)
        total = jnp.zeros((8, TILE), f32)
        for i in range(BLOCK // TILE):
            rows = slice(i * TILE, (i + 1) * TILE)
            if final:
                part_h = jnp.dot(lr[i].reshape(TILE, BLOCK), block, preferred_element_type=f32).astype(bf16)
            else:
                part_h = h[rows]
            for j in range(BLOCK // TILE):
                cut = slice(j * TILE, (j + 1) * TILE)
                p = jnp.dot(part_h, rr[pair, cut], preferred_element_type=f32)
                if m:
                    p += full[rows, cut]
                full[rows, cut] = p
                if final:
                    total += jnp.sum((p * p).reshape(TILE // 8, 8, TILE), axis=0)
            if final and i == 0:
                cut_rows(0, None)
                spread(0)
        return total

    for k, (c0, r0, n) in enumerate(CHUNKS):
        drain(s1[k], rs1.at[k])
        for i, d in enumerate(ts):
            s2[k][i] = r1[k][lines[i]]
            send(s2[k].at[i], g.at[:, t, pl.ds(r0, n), c0 : c0 + CW], ss2.at[k], rs2.at[k], f, d)
        g[:, t, r0 : r0 + n, c0 : c0 + CW] = r1[k][my_line]
        if k == 4:
            for load in big[:5]:
                load.wait()
        for m in range(BLOCK // PAIR - 1):
            if k == max(j for j in range(FWD) if CHUNKS[j][0] // PAIR == m) + 3:
                products(m)
                turn(m)
    total = products(BLOCK // PAIR - 1)
    factor = lax.rsqrt(jnp.sum(total, axis=(0, 1), keepdims=True) / (BLOCK * BLOCK) + eps)

    fac_out[...] = jnp.broadcast_to(factor, fac_out.shape)
    for d in ts:
        send(fac_out, fac.at[t], sf, rf_sem, f, d)
    fac[t] = jnp.broadcast_to(factor, fac_out.shape)
    for c in range(1, BWD):
        r, c0, _ = BACK[c]
        if r and not c0:
            cut_rows(r, factor)
        spread(c)

    def scaled(piece, slot, c):
        if BACK[c][0]:
            return piece
        scale = jnp.concatenate([fac[slot][0:1]] * (BACK[c][2] // 128), axis=1)
        return (piece.astype(f32) * scale).astype(bf16)


    def left(i):
        rows = pl.ds(i * TILE, TILE)
        a = rows_of(g, i)
        for j in range(BLOCK // TILE):
            cut = slice(j * TILE, (j + 1) * TILE)
            p = jnp.dot(a, gt[:, cut], preferred_element_type=f32)
            nl[rows, cut] = decay * nl[rows, cut] + jnp.where(has, (1.0 - decay) * p, 0.0)

    def right(i):
        rows = pl.ds(i * TILE, TILE)
        a = gt[rows]
        for j in range(BLOCK // TILE):
            cut = slice(j * TILE, (j + 1) * TILE)
            p = jnp.dot(a, g[:, :, :, cut].reshape(BLOCK, TILE), preferred_element_type=f32)
            nr[rows, cut] = decay * nr[rows, cut] + jnp.where(has, (1.0 - decay) * p, 0.0)

    turn(BLOCK // PAIR - 1)
    for load in big[5:]:
        load.wait()
    work = [lambda i=i: left(i) for i in range(4)] + [lambda i=i: right(i) for i in range(4)]
    work.pop(0)()
    work.pop(0)()

    def parts_of(tp):
        parts = []
        for j in range(OUT_COLS // Q):
            chunk = tp * (OUT_COLS // Q) + j
            parts.append((owner_ref[line * COLS + chunk // (BLOCK // Q)] >> 3, chunk % (BLOCK // Q)))
        return parts

    sources = [slots[N_T + d // 2] for d in fs]
    my_source = slots[N_T + line]
    parts = [parts_of(d) for d in ts]
    my_parts = parts_of(t)

    def finish(r):
        for c in range(BWD):
            if BACK[c][0] == r:
                drain(b2[c], rx_sem.at[c])
        here = pl.ds(pl.multiple_of(t * ROWS + r * RW, RW), RW)
        for i, d in enumerate(ts):
            for j, (source, q) in enumerate(parts[i]):
                b3[r, i, :, j * Q : (j + 1) * Q] = rx[r][source, q]
            send(b3.at[r, i], upd.at[here], sz.at[r], rz_sem.at[r], f, d)
        for j, (source, q) in enumerate(my_parts):
            upd[here, j * Q : (j + 1) * Q] = rx[r][source, q]

    for c, (r, c0, width) in enumerate(BACK):
        drain(ra[c].at[pl.ds(0, NT)], ra_sem.at[c])
        if c == 0:
            drain(fac.at[pl.ds(0, NT)], rf_sem)
        first, count = c0 // Q, width // Q
        for i, d in enumerate(fs):
            piece = scaled(ra[c][sources[i], d % 2], sources[i], c)
            for q in range(count):
                b2[c][i, q] = piece[:, q * Q : (q + 1) * Q]
            send(b2[c].at[i], rx[r].at[f, pl.ds(first, count)], sx.at[c], rx_sem.at[c], d, t)
        piece = scaled(ra[c][my_source, part], my_source, c)
        for q in range(count):
            rx[r][f, first + q] = piece[:, q * Q : (q + 1) * Q]
        if r and c0 + width == BLOCK:
            finish(r - 1)
        if work:
            work.pop(0)()
    finish(GROUPS - 1)

    for k in range(FWD):
        drain(s1[k], ss1.at[k])
        drain(s2[k], ss2.at[k])
    for c in range(BWD):
        drain(ra[c].at[pl.ds(0, NT)], sa.at[c])
        drain(b2[c], sx.at[c])
    drain(fac.at[pl.ds(0, NT)], sf)
    for r in range(GROUPS):
        drain(b3.at[r], sz.at[r])
        drain(b3.at[r], rz_sem.at[r])


def step(owner, gradient, l_stat, r_stat, l_root, r_root):
    hbm = pl.BlockSpec(memory_space=pltpu.HBM)
    vmem = pl.BlockSpec(memory_space=VMEM)
    return pl.pallas_call(
        kernel,
        out_shape=[
            VMEM((N_T * ROWS, OUT_COLS), bf16),
            VMEM((BLOCK, BLOCK), f32),
            VMEM((BLOCK, BLOCK), f32),
        ],
        in_specs=[hbm] * 6,
        out_specs=[vmem] * 3,
        scratch_shapes=[
            VMEM((COLS, ROWS, BLOCK), bf16),
            VMEM((GROUPS, 2, N_T, RW, BLOCK), bf16),
            VMEM((BLOCK, BLOCK), bf16),
            VMEM((2, N_T, ROWS, BLOCK), bf16),
            VMEM((BLOCK, BLOCK), bf16),
            VMEM((BLOCK, BLOCK), f32),
            VMEM((2, N_T, ROWS, BLOCK), bf16),
            VMEM((GROUPS, NT, RW, OUT_COLS), bf16),
            VMEM((N_T, 8, 128), f32),
            VMEM((8, 128), f32),
            pltpu.SMEM((LINES * COLS,), jnp.int32),
            pltpu.SMEM((N_T + LINES,), jnp.int32),
        ]
        + [VMEM((NF, n, CW), bf16) for _, _, n in CHUNKS]
        + [VMEM((NT, 2, n, CW), bf16) for _, _, n in CHUNKS]
        + [VMEM((LINES, 2, n, CW), bf16) for _, _, n in CHUNKS]
        + [VMEM((N_T, 2, RW, w), bf16) for _, _, w in BACK]
        + [VMEM((NF, w // Q, RW, Q), bf16) for _, _, w in BACK]
        + [VMEM((N_F, BLOCK // Q, RW, Q), bf16)] * GROUPS
        + [DMA((COLS,)), DMA((5 + GROUPS,))]
        + [DMA((FWD,))] * 4
        + [DMA((BWD,))] * 4
        + [DMA((GROUPS,))] * 2
        + [DMA] * 2,
        compiler_params=pltpu.CompilerParams(collective_id=0, has_side_effects=True, vmem_limit_bytes=40 << 20),
        name="shampoo",
    )(owner, gradient, l_stat, r_stat, l_root, r_root)


def write_kernel(a, b, c, oa, ob, oc, sems):
    copies = [pltpu.make_async_copy(x, y, sems.at[i]) for i, (x, y) in enumerate([(a, oa), (b, ob), (c, oc)])]
    for copy in copies:
        copy.start()
    for copy in copies:
        copy.wait()


def write(update, new_left, new_right):
    outs = (update, new_left, new_right)
    return pl.pallas_call(
        write_kernel,
        out_shape=[jax.ShapeDtypeStruct(x.shape, x.dtype) for x in outs],
        in_specs=[pl.BlockSpec(memory_space=VMEM)] * 3,
        out_specs=[pl.BlockSpec(memory_space=pltpu.HBM)] * 3,
        scratch_shapes=[DMA((3,))],
        compiler_params=pltpu.CompilerParams(vmem_limit_bytes=16 << 20),
        name="write",
    )(*outs)


def per_device(gradient, owner, l_stat, r_stat, l_root, r_root):
    args = (owner, gradient, l_stat[0], r_stat[0], l_root.reshape(2, N_T, GROUPS, RW, BLOCK), r_root[0])
    args = [pltpu.with_memory_space_constraint(x, pltpu.HBM) for x in args]
    update, new_left, new_right = write(*step(*args))
    return (update, new_left[None], new_right[None])


def solution(mesh):
    stat = P(("fsdp", "tp"), None, None)
    return jax.shard_map(
        per_device,
        mesh=mesh,
        in_specs=(P(("fsdp", "tp"), None), P(), stat, stat, stat, stat),
        out_specs=(P("fsdp", "tp"), stat, stat),
        check_vma=False,
    )
```

```python
import jax
import jax.numpy as jnp
from jax import lax
from jax.experimental import pallas as pl
from jax.experimental.pallas import tpu as pltpu
from jax.sharding import PartitionSpec as P

MESH = pl.DeviceIdType.MESH
VMEM = pltpu.VMEM
DMA = pltpu.SemaphoreType.DMA
f32, bf16 = jnp.float32, jnp.bfloat16

decay = 0.9
eps = 1e-06

BLOCK = 1024
LINES = 8
COLS = 10
N_F = 16
N_T = 8
RING = 4
ROWS = 64
CW = 128
CHUNKS = [(0, 0, 32), (0, 32, 32)]
CHUNKS += [(c, 0, 64) for c in range(CW, BLOCK - CW, CW)]
CHUNKS += [(BLOCK - CW, 0, 32), (BLOCK - CW, 32, 32)]
FWD = len(CHUNKS)
STAGED = 2
PAIR = 256
RW = 16
GROUPS = ROWS // RW
OUT_COLS = 1280
Q = 256
TILE = 256
BACK = [(0, 0, 512), (0, 512, 512)] + [(r, c, 512) for r in range(1, GROUPS) for c in (0, 512)]
BWD = len(BACK)

F_STEPS = [(2, 2), (1, 2), (2, 1), (3, 2), (2, 3), (1, 1), (3, 3), (1, 3), (3, 1), (0, 2), (2, 0), (0, 1), (1, 0), (0, 3), (3, 0)]
T_STEPS = [(2, 0), (2, 1), (1, 0), (3, 0), (1, 1), (3, 1), (0, 1)]
NF, NT = len(F_STEPS), len(T_STEPS)
Z_STEPS = [(2, 0), (1, 0), (3, 0)]
NZ = len(Z_STEPS)
DIRECT = 2


def fsdp_at(f, step):
    y = (f // RING + step[0]) % RING
    x = (f % RING + step[1]) % RING
    return y * RING + x


def tp_at(t, step):
    return ((t // 2 + step[0]) % RING) * 2 + (t % 2 + step[1]) % 2


def send(src, dst, send_sem, recv_sem, f, t):
    pltpu.make_async_remote_copy(
        src_ref=src, dst_ref=dst, send_sem=send_sem, recv_sem=recv_sem, device_id=(f, t), device_id_type=MESH
    ).start()


def drain(like, sem):
    pltpu.make_async_copy(like, like, sem).wait()


def rows_of(ref, i):
    return ref[i // 2, pl.ds((i % 2) * 4, 4)].reshape(TILE, ref.shape[-1])


def kernel(owner_hbm, g_hbm, ls_hbm, rs_hbm, lr_hbm, rr_hbm, upd, nl, nr, *scratch):
    scratch = list(scratch)

    def take(n):
        taken, scratch[:n] = scratch[:n], []
        return taken

    gv, lr, rr, g, gt, full, s, b3, fac, fac_out, owner_ref, slots = take(12)
    s1, s2, r1, ra, rl, b2, rx = take(FWD), take(FWD), take(FWD), take(BWD), take(BWD), take(BWD), take(GROUPS)
    last = take(GROUPS - 1)
    gsem, lsem, ss1, rs1, ss2, rs2, sa, ra_sem, sx, rx_sem, sz, rz_sem, sf, rf_sem, sl, rl_sem, sl_last, last_sem = scratch

    f, t = lax.axis_index("fsdp"), lax.axis_index("tp")
    line, part = f // 2, f % 2
    fs = [fsdp_at(f, step) for step in F_STEPS]
    ts = [tp_at(t, step) for step in T_STEPS]
    zs = [tp_at(t, step) for step in Z_STEPS]
    other = tp_at(t, (0, 1))

    names = pltpu.make_async_copy(owner_hbm, owner_ref, lsem.at[4])
    names.start()
    barrier = pltpu.get_barrier_semaphore()
    for d in fs:
        pl.semaphore_signal(barrier, inc=1, device_id=(d, t), device_id_type=MESH)
    for d in ts:
        pl.semaphore_signal(barrier, inc=1, device_id=(f, d), device_id_type=MESH)

    loads = [pltpu.make_async_copy(g_hbm.at[:, c * BLOCK : (c + 1) * BLOCK], gv.at[c], gsem.at[c]) for c in range(COLS)]
    big = [
        pltpu.make_async_copy(lr_hbm.at[:, :, r], lr.at[r], lsem.at[5 + r]) for r in range(GROUPS)
    ] + [
        pltpu.make_async_copy(rr_hbm, rr, lsem.at[1]),
        pltpu.make_async_copy(ls_hbm, nl, lsem.at[2]),
        pltpu.make_async_copy(rs_hbm, nr, lsem.at[3]),
    ]
    for load in loads:
        load.start()
    names.wait()

    near = [owner_ref[line * COLS + c] >> 3 for c in range(COLS)]

    def column_of(fsdp):
        col = jnp.int32(0)
        for c in range(COLS):
            col = jnp.where(near[c] == fsdp, c, col)
        return col

    cols = [column_of(d) for d in fs]
    my_col = column_of(f)
    for load in loads:
        load.wait()

    def stage(k):
        c0, r0, n = CHUNKS[k]
        for i in range(NF):
            s1[k][i] = gv[cols[i], r0 : r0 + n, c0 : c0 + CW]
        r1[k][line, part] = gv[my_col, r0 : r0 + n, c0 : c0 + CW]

    for k in range(STAGED):
        stage(k)
    pl.semaphore_wait(barrier, NF + NT)
    for k in range(FWD):
        if k >= STAGED:
            stage(k)
        for i, d in enumerate(fs):
            send(s1[k].at[i], r1[k].at[line, part], ss1.at[k], rs1.at[k], d, t)
        if k == 1:
            for load in big:
                load.start()

    owned = [jnp.int32(-1)] * N_T
    for r in range(LINES):
        tp = jnp.int32(0)
        for c in range(COLS):
            o = owner_ref[r * COLS + c]
            here = (o >> 3) == f
            low = o & 7
            tp = jnp.where(here, low, tp)
            away = jnp.where(here, low, -1)
            owned = [jnp.where(away == p, r, owned[p]) for p in range(N_T)]
        slots[N_T + r] = tp
    for p in range(N_T):
        slots[p] = owned[p]
    mine = slots[t]
    has = mine >= 0
    lines = [jnp.maximum(slots[d], 0) for d in ts]
    my_line = jnp.maximum(mine, 0)

    def cut_rows(r, factor):
        for h in range(2):
            for p in range(N_T):
                start = r * TILE + (h * N_T + p) * RW
                rows = full[start : start + RW]
                s[h, p, r * RW : (r + 1) * RW] = (rows if factor is None else rows * factor).astype(bf16)

    def spread(c):
        r, c0, width = BACK[c]
        rows, cut = pl.ds(r * RW, RW), pl.ds(c0, width)
        for j, d in enumerate(zs):
            if c < DIRECT:
                send(s.at[:, d + other - t, rows, cut], ra[c].at[t], sa.at[c], ra_sem.at[c], f, d + other - t)
            else:
                send(s.at[:, d + other - t, rows, cut], rl[c].at[j], sl.at[c], rl_sem.at[c], f, other)
        send(s.at[:, other, rows, cut], ra[c].at[t], sa.at[c], ra_sem.at[c], f, other)
        for d in zs:
            send(s.at[:, d, rows, cut], ra[c].at[t], sa.at[c], ra_sem.at[c], f, d)
        ra[c][t] = s[:, t, rows, cut]

    def relay(c):
        drain(rl[c], rl_sem.at[c])
        for j, d in enumerate(zs):
            send(rl[c].at[j], ra[c].at[other], sa.at[c], ra_sem.at[c], f, d)

    def turn(m):
        pair = slice(m * PAIR, (m + 1) * PAIR)
        gt[pair, :] = g[:, :, :, pair].reshape(BLOCK, PAIR).T

    def products(m):
        pair = slice(m * PAIR, (m + 1) * PAIR)
        for k, (c0, _, _) in enumerate(CHUNKS):
            if c0 // PAIR == m:
                drain(s2[k], rs2.at[k])
        block = g[:, :, :, pair].reshape(BLOCK, PAIR)
        final = m == BLOCK // PAIR - 1
        if not final:
            h = jnp.dot(lr[...].reshape(BLOCK, BLOCK), block, preferred_element_type=f32).astype(bf16)
        total = jnp.zeros((8, TILE), f32)
        for i in range(BLOCK // TILE):
            rows = slice(i * TILE, (i + 1) * TILE)
            if final:
                part_h = jnp.dot(lr[i].reshape(TILE, BLOCK), block, preferred_element_type=f32).astype(bf16)
            else:
                part_h = h[rows]
            for j in range(BLOCK // TILE):
                cut = slice(j * TILE, (j + 1) * TILE)
                p = jnp.dot(part_h, rr[pair, cut], preferred_element_type=f32)
                if m:
                    p += full[rows, cut]
                full[rows, cut] = p
                if final:
                    total += jnp.sum((p * p).reshape(TILE // 8, 8, TILE), axis=0)
            if final and i == 0:
                cut_rows(0, None)
                spread(0)
        return total

    for k, (c0, r0, n) in enumerate(CHUNKS):
        drain(s1[k], rs1.at[k])
        for i, d in enumerate(ts):
            s2[k][i] = r1[k][lines[i]]
            send(s2[k].at[i], g.at[:, t, pl.ds(r0, n), c0 : c0 + CW], ss2.at[k], rs2.at[k], f, d)
        g[:, t, r0 : r0 + n, c0 : c0 + CW] = r1[k][my_line]
        if k == 4:
            for load in big[:5]:
                load.wait()
        for m in range(BLOCK // PAIR - 1):
            if k == max(j for j in range(FWD) if CHUNKS[j][0] // PAIR == m) + 3:
                products(m)
                turn(m)
    total = products(BLOCK // PAIR - 1)
    factor = lax.rsqrt(jnp.sum(total, axis=(0, 1), keepdims=True) / (BLOCK * BLOCK) + eps)

    fac_out[...] = jnp.broadcast_to(factor, fac_out.shape)
    for d in ts:
        send(fac_out, fac.at[t], sf, rf_sem, f, d)
    fac[t] = jnp.broadcast_to(factor, fac_out.shape)
    for c in range(1, BWD):
        r, c0, _ = BACK[c]
        if r and not c0:
            cut_rows(r, factor)
        spread(c)
        if c > DIRECT:
            relay(c - 1)
    relay(BWD - 1)

    def scaled(piece, slot, c):
        if BACK[c][0]:
            return piece
        scale = jnp.concatenate([fac[slot][0:1]] * (BACK[c][2] // 128), axis=1)
        return (piece.astype(f32) * scale).astype(bf16)


    def left(i):
        rows = pl.ds(i * TILE, TILE)
        a = rows_of(g, i)
        for j in range(BLOCK // TILE):
            cut = slice(j * TILE, (j + 1) * TILE)
            p = jnp.dot(a, gt[:, cut], preferred_element_type=f32)
            nl[rows, cut] = decay * nl[rows, cut] + jnp.where(has, (1.0 - decay) * p, 0.0)

    def right(i):
        rows = pl.ds(i * TILE, TILE)
        a = gt[rows]
        for j in range(BLOCK // TILE):
            cut = slice(j * TILE, (j + 1) * TILE)
            p = jnp.dot(a, g[:, :, :, cut].reshape(BLOCK, TILE), preferred_element_type=f32)
            nr[rows, cut] = decay * nr[rows, cut] + jnp.where(has, (1.0 - decay) * p, 0.0)

    turn(BLOCK // PAIR - 1)
    for load in big[5:]:
        load.wait()
    work = [lambda i=i: left(i) for i in range(4)] + [lambda i=i: right(i) for i in range(4)]
    work.pop(0)()
    work.pop(0)()

    def parts_of(tp):
        parts = []
        for j in range(OUT_COLS // Q):
            chunk = tp * (OUT_COLS // Q) + j
            parts.append((owner_ref[line * COLS + chunk // (BLOCK // Q)] >> 3, chunk % (BLOCK // Q)))
        return parts

    sources = [slots[N_T + d // 2] for d in fs]
    my_source = slots[N_T + line]
    parts = [parts_of(d) for d in ts]
    my_parts = parts_of(t)

    def finish(r):
        for c in range(BWD):
            if BACK[c][0] == r:
                drain(b2[c], rx_sem.at[c])
        here = pl.ds(pl.multiple_of(t * ROWS + r * RW, RW), RW)
        for i, d in enumerate(ts):
            for j, (source, q) in enumerate(parts[i]):
                b3[r, i, :, j * Q : (j + 1) * Q] = rx[r][source, q]
            z, core = T_STEPS[i]
            if core and z and r < GROUPS - 1:
                send(b3.at[r, i], last[r].at[Z_STEPS.index((z, 0))], sz.at[r], last_sem.at[r], f, other)
            else:
                send(b3.at[r, i], upd.at[here], sz.at[r], rz_sem.at[r], f, d)
        for j, (source, q) in enumerate(my_parts):
            upd[here, j * Q : (j + 1) * Q] = rx[r][source, q]

    def relay_last(r):
        drain(last[r], last_sem.at[r])
        there = pl.ds(pl.multiple_of(other * ROWS + r * RW, RW), RW)
        for j, d in enumerate(zs):
            send(last[r].at[j], upd.at[there], sl_last.at[r], rz_sem.at[r], f, d)

    for c, (r, c0, width) in enumerate(BACK):
        drain(ra[c].at[pl.ds(0, NT)], ra_sem.at[c])
        if c == 0:
            drain(fac.at[pl.ds(0, NT)], rf_sem)
        first, count = c0 // Q, width // Q
        for i, d in enumerate(fs):
            piece = scaled(ra[c][sources[i], d % 2], sources[i], c)
            for q in range(count):
                b2[c][i, q] = piece[:, q * Q : (q + 1) * Q]
            send(b2[c].at[i], rx[r].at[f, pl.ds(first, count)], sx.at[c], rx_sem.at[c], d, t)
        piece = scaled(ra[c][my_source, part], my_source, c)
        for q in range(count):
            rx[r][f, first + q] = piece[:, q * Q : (q + 1) * Q]
        if r and c0 + width == BLOCK:
            finish(r - 1)
            relay_last(r - 1)
        if work:
            work.pop(0)()
    finish(GROUPS - 1)

    for k in range(FWD):
        drain(s1[k], ss1.at[k])
        drain(s2[k], ss2.at[k])
    for c in range(BWD):
        drain(ra[c].at[pl.ds(0, NT)], sa.at[c])
        if c >= DIRECT:
            drain(rl[c], sl.at[c])
        drain(b2[c], sx.at[c])
    drain(fac.at[pl.ds(0, NT)], sf)
    for r in range(GROUPS - 1):
        drain(last[r], sl_last.at[r])
    for r in range(GROUPS):
        drain(b3.at[r], sz.at[r])
        drain(b3.at[r], rz_sem.at[r])


def step(owner, gradient, l_stat, r_stat, l_root, r_root):
    hbm = pl.BlockSpec(memory_space=pltpu.HBM)
    vmem = pl.BlockSpec(memory_space=VMEM)
    return pl.pallas_call(
        kernel,
        out_shape=[
            VMEM((N_T * ROWS, OUT_COLS), bf16),
            VMEM((BLOCK, BLOCK), f32),
            VMEM((BLOCK, BLOCK), f32),
        ],
        in_specs=[hbm] * 6,
        out_specs=[vmem] * 3,
        scratch_shapes=[
            VMEM((COLS, ROWS, BLOCK), bf16),
            VMEM((GROUPS, 2, N_T, RW, BLOCK), bf16),
            VMEM((BLOCK, BLOCK), bf16),
            VMEM((2, N_T, ROWS, BLOCK), bf16),
            VMEM((BLOCK, BLOCK), bf16),
            VMEM((BLOCK, BLOCK), f32),
            VMEM((2, N_T, ROWS, BLOCK), bf16),
            VMEM((GROUPS, NT, RW, OUT_COLS), bf16),
            VMEM((N_T, 8, 128), f32),
            VMEM((8, 128), f32),
            pltpu.SMEM((LINES * COLS,), jnp.int32),
            pltpu.SMEM((N_T + LINES,), jnp.int32),
        ]
        + [VMEM((NF, n, CW), bf16) for _, _, n in CHUNKS]
        + [VMEM((NT, 2, n, CW), bf16) for _, _, n in CHUNKS]
        + [VMEM((LINES, 2, n, CW), bf16) for _, _, n in CHUNKS]
        + [VMEM((N_T, 2, RW, w), bf16) for _, _, w in BACK]
        + [VMEM((NZ, 2, RW, w), bf16) for _, _, w in BACK]
        + [VMEM((NF, w // Q, RW, Q), bf16) for _, _, w in BACK]
        + [VMEM((N_F, BLOCK // Q, RW, Q), bf16)] * GROUPS
        + [VMEM((NZ, RW, OUT_COLS), bf16)] * (GROUPS - 1)
        + [DMA((COLS,)), DMA((5 + GROUPS,))]
        + [DMA((FWD,))] * 4
        + [DMA((BWD,))] * 4
        + [DMA((GROUPS,))] * 2
        + [DMA] * 2
        + [DMA((BWD,))] * 2
        + [DMA((GROUPS,))] * 2,
        compiler_params=pltpu.CompilerParams(collective_id=0, has_side_effects=True, vmem_limit_bytes=40 << 20),
        name="shampoo",
    )(owner, gradient, l_stat, r_stat, l_root, r_root)


def write_kernel(a, b, c, oa, ob, oc, sems):
    copies = [pltpu.make_async_copy(x, y, sems.at[i]) for i, (x, y) in enumerate([(a, oa), (b, ob), (c, oc)])]
    for copy in copies:
        copy.start()
    for copy in copies:
        copy.wait()


def write(update, new_left, new_right):
    outs = (update, new_left, new_right)
    return pl.pallas_call(
        write_kernel,
        out_shape=[jax.ShapeDtypeStruct(x.shape, x.dtype) for x in outs],
        in_specs=[pl.BlockSpec(memory_space=VMEM)] * 3,
        out_specs=[pl.BlockSpec(memory_space=pltpu.HBM)] * 3,
        scratch_shapes=[DMA((3,))],
        compiler_params=pltpu.CompilerParams(vmem_limit_bytes=16 << 20),
        name="write",
    )(*outs)


def per_device(gradient, owner, l_stat, r_stat, l_root, r_root):
    args = (owner, gradient, l_stat[0], r_stat[0], l_root.reshape(2, N_T, GROUPS, RW, BLOCK), r_root[0])
    args = [pltpu.with_memory_space_constraint(x, pltpu.HBM) for x in args]
    update, new_left, new_right = write(*step(*args))
    return (update, new_left[None], new_right[None])


def solution(mesh):
    stat = P(("fsdp", "tp"), None, None)
    return jax.shard_map(
        per_device,
        mesh=mesh,
        in_specs=(P(("fsdp", "tp"), None), P(), stat, stat, stat, stat),
        out_specs=(P("fsdp", "tp"), stat, stat),
        check_vma=False,
    )
```
